512 devices in a mesh: ctx: 128 (over z, x, core), grp: 4 (over y).
Axes of the slice: x: 4, y: 4, z: 16, core: 2. Of those that a mesh axis runs over, the one named last changes fastest.
Arguments:
- queries: bfloat16 [16384, 12288], P('ctx', 'grp'), parts along dimension 1, may hold values from -250 to 250
- keys: bfloat16 [2, 16384, 768], P(None, 'ctx', 'grp'), parts along dimension 2, may hold values from -6 to 6
- values: bfloat16 [2, 16384, 512], P(None, 'ctx', 'grp'), parts along dimension 2, may hold values from -6 to 6
- gate_logits: bfloat16 [16384, 192], P('ctx', 'grp'), parts along dimension 1, may hold values from -6 to 6
- sel_ids: int32 [1024, 64], P('ctx', 'grp'), parts along dimension 1, may hold values from -1 to 511, as said below
- pos_k: bfloat16 [32, 768], P(None, 'grp'), parts along dimension 1, may hold values from -1 to 1
- pos_v: bfloat16 [32, 512], P(None, 'grp'), parts along dimension 1, may hold values from -1 to 1
- mix_k: bfloat16 [192, 768], P(None, 'grp'), parts along dimension 1, may hold values from -0.4375 to 0.4375
- mix_v: bfloat16 [128, 512], P(None, 'grp'), parts along dimension 1, may hold values from -0.5 to 0.5
Outputs:
- attended: bfloat16 [16384, 8192], P('ctx', 'grp'), parts along dimension 1
The draws below stay inside these ranges and needn't reach their ends.
There are 4 independent parts, one for each index of `grp`. The reference program is written for one: setup_inputs(seed, part) draws one part's arguments, and reference() takes and returns one part's arrays. A program takes and returns all parts, laid end to end along the dimension named above; each array names one. Nothing has to cross between parts.
Inputs may be any that keep to these rules, and one draw needn't show every extreme that they name: `sel_ids`: the first entry of a row is the block that holds the row's tokens. The other entries name distinct blocks that lie wholly before position 16384, or are -1 at the row's end; each row has at least 12 entries that are not -1. Over the 8 rows of one device, the entries after the first name at most 64 = min(64, 1 * 2 * 128) distinct blocks, at most 1 of them held by one device, and no block in more than 2 rows.
All inputs are finite; a program needn't handle non-finite values.
Results may differ from the reference program's by a relative error of at most 0.011.
Values may be sent and summed in bfloat16 or wider, within the bound.
A program may use at most 128 MiB of HBM per device.

```python
import jax
import jax.numpy as jnp
from jax import lax

HEADS = 16
DK = 192
DV = 128
CMP_BLOCK = 32
SEL_BLOCK = 64
TOPN = 16
QRY_DEV = 128
QBLOCK = 16
CACHE_ROUNDS = 1
SPAN = 16384
ROUNDS = 2
CONTEXT = 32768
WINDOW = 512
BPP = 2
NBLK = 512
QB_DEV = 8
UNIQ = 64
N_CTX = 128


def draw_queries(key, part):
    normal_key = jax.random.fold_in(jax.random.fold_in(key, 11), 0)
    entries = jax.random.normal(normal_key, (SPAN, HEADS * DK), jnp.float32)
    entries = jnp.clip(entries, -6.0, 6.0)
    return entries.astype(jnp.bfloat16)


def draw_sel_ids(key, part):
    device_keys = jax.random.split(jax.random.fold_in(key, 23), N_CTX)

    def one_device(device_key, device_no):
        perm_key, base_key, count_key = jax.random.split(device_key, 3)
        holders = jax.random.permutation(perm_key, N_CTX)
        starts = jax.random.randint(base_key, (N_CTX,), 0, CACHE_ROUNDS * BPP)
        counts = jax.random.randint(count_key, (QB_DEV,), TOPN - TOPN // 4, TOPN + 1)
        counts = counts.at[0].set(TOPN)
        row_no = jnp.arange(QB_DEV)[:, None]
        column = jnp.arange(1, TOPN)[None, :]
        label_no = (row_no * (TOPN - 1) + column - 1) % UNIQ
        holder = holders[label_no % N_CTX]
        local_no = (starts[holder] + label_no // N_CTX) % (CACHE_ROUNDS * BPP)
        block_no = (local_no // BPP * N_CTX + holder) * BPP + local_no % BPP
        block_no = jnp.where(column < counts[:, None], block_no, -1)
        own_block = (CACHE_ROUNDS * SPAN + device_no * QRY_DEV + jnp.arange(QB_DEV) * QBLOCK) // SEL_BLOCK
        return jnp.concatenate([own_block[:, None], block_no], axis=1).astype(jnp.int32)
    table = jax.vmap(one_device)(device_keys, jnp.arange(N_CTX))
    return table.reshape(SPAN // QBLOCK, TOPN)


def block_levels(rng, shape, cuts, least, largest):
    loudness, own = 1.0, jax.random.fold_in(rng, 6)
    for axis_at, parts in cuts:
        draws = jnp.exp(jax.random.uniform(jax.random.fold_in(own, axis_at), (parts,), jnp.float32, least / len(cuts), largest / len(cuts)))
        loudness = loudness * jnp.repeat(draws, shape[axis_at] // parts).reshape([-1 if axis == axis_at else 1 for axis in range(len(shape))])
    return loudness


def centred(own_key, dims, scale, most, pieces=(), kind=jnp.bfloat16):
    array = jax.random.normal(own_key, dims, jnp.float32) * scale
    if len(pieces) > 0:
        array = block_levels(own_key, dims, pieces, -0.22, 0.18) * array
    return jnp.clip(array, min=-most, max=most).astype(kind)


def setup_inputs(seed: int = 0, part: int = 0) -> dict:
    key_list = jax.random.split(jax.random.key(seed), 10)
    part_keys = jax.random.split(jax.random.fold_in(key_list[9], part), 10)
    return {
        "queries": draw_queries(jax.random.fold_in(jax.random.fold_in(key_list[9], part), 71), part),
        "keys": centred(part_keys[1], (ROUNDS, SPAN, DK), 1.0, 6.0, ((1, 128),)),
        "values": centred(part_keys[2], (ROUNDS, SPAN, DV), 1.0, 6.0, ((1, 128),)),
        "gate_logits": centred(part_keys[3], (SPAN, 3 * HEADS), 1.5, 6.0, ((0, 128),)),
        "sel_ids": draw_sel_ids(jax.random.fold_in(jax.random.fold_in(key_list[9], part), 71), part),
        "pos_k": centred(part_keys[5], (CMP_BLOCK, DK), CMP_BLOCK ** -0.5, 1.0),
        "pos_v": centred(part_keys[6], (CMP_BLOCK, DV), CMP_BLOCK ** -0.5, 1.0),
        "mix_k": centred(part_keys[7], (DK, DK), DK ** -0.5, 0.4375),
        "mix_v": centred(part_keys[8], (DV, DV), DV ** -0.5, 0.5),
    }


def attention(query_rows, key_rows, value_rows, allowed, head_count):
    scores = jnp.dot(query_rows, key_rows.T, preferred_element_type=jnp.float32) * (query_rows.shape[1] ** -0.5)
    scores = scores.reshape(-1, head_count, key_rows.shape[0])
    scores = jnp.where(allowed[:, None, :], scores, -jnp.inf)
    highest = jnp.max(scores, axis=2, keepdims=True)
    weights = jnp.exp(scores - highest)
    totals = jnp.sum(weights, axis=2)
    rounded = weights.astype(jnp.bfloat16).reshape(-1, key_rows.shape[0])
    mixture = jnp.dot(rounded, value_rows, preferred_element_type=jnp.float32)
    return mixture.reshape(-1, head_count, value_rows.shape[1]) / totals[:, :, None]


def compress(rows, gains, mixing):
    count = rows.shape[0] // CMP_BLOCK
    blocks = rows.reshape(count, CMP_BLOCK, rows.shape[1]).astype(jnp.float32)
    pooled = jnp.einsum("bjd,jd->bd", blocks, gains.astype(jnp.float32)).astype(jnp.bfloat16)
    return jnp.dot(pooled, mixing, preferred_element_type=jnp.float32).astype(jnp.bfloat16)


def reference(queries, keys, values, gate_logits, sel_ids, pos_k, pos_v, mix_k, mix_v):
    key_flat = keys.reshape(CONTEXT, DK)
    value_flat = values.reshape(CONTEXT, DV)
    first_query = CACHE_ROUNDS * SPAN
    comp_keys = compress(key_flat, pos_k, mix_k)
    comp_values = compress(value_flat, pos_v, mix_v)
    comp_ends = jnp.arange(CONTEXT // CMP_BLOCK, dtype=jnp.int32) * CMP_BLOCK + (CMP_BLOCK - 1)
    rows_each = min(512, SPAN)

    def dense_branches(block_no):
        offset = (block_no * rows_each).astype(jnp.int32)
        query_rows = lax.dynamic_slice_in_dim(queries, offset, rows_each, 0).reshape(rows_each * HEADS, DK)
        query_pos = first_query + offset + jnp.arange(rows_each, dtype=jnp.int32)
        compressed = attention(query_rows, comp_keys, comp_values, comp_ends[None, :] <= query_pos[:, None], HEADS)
        window_start = (first_query + offset - WINDOW).astype(jnp.int32)
        near_keys = lax.dynamic_slice_in_dim(key_flat, window_start, rows_each + WINDOW, 0)
        near_values = lax.dynamic_slice_in_dim(value_flat, window_start, rows_each + WINDOW, 0)
        key_pos = window_start + jnp.arange(rows_each + WINDOW, dtype=jnp.int32)
        inside = (key_pos[None, :] <= query_pos[:, None]) & (key_pos[None, :] > query_pos[:, None] - WINDOW)
        sliding = attention(query_rows, near_keys, near_values, inside, HEADS)
        return compressed, sliding

    compressed, sliding = lax.map(dense_branches, jnp.arange(SPAN // rows_each, dtype=jnp.int32))
    compressed = compressed.reshape(SPAN, HEADS, DV)
    sliding = sliding.reshape(SPAN, HEADS, DV)
    key_blocks = key_flat.reshape(NBLK, SEL_BLOCK, DK)
    value_blocks = value_flat.reshape(NBLK, SEL_BLOCK, DV)

    def selected_branch(block_no):
        chosen = sel_ids[block_no]
        clipped = jnp.maximum(chosen, 0).astype(jnp.int32)
        near_keys = key_blocks[clipped].reshape(TOPN * SEL_BLOCK, DK)
        near_values = value_blocks[clipped].reshape(TOPN * SEL_BLOCK, DV)
        offset = (block_no * QBLOCK).astype(jnp.int32)
        query_rows = lax.dynamic_slice_in_dim(queries, offset, QBLOCK, 0).reshape(QBLOCK * HEADS, DK)
        query_pos = first_query + offset + jnp.arange(QBLOCK, dtype=jnp.int32)
        key_pos = (clipped[:, None] * SEL_BLOCK + jnp.arange(SEL_BLOCK, dtype=jnp.int32)[None, :]).reshape(-1)
        usable = jnp.repeat(chosen >= 0, SEL_BLOCK)
        allowed = usable[None, :] & (key_pos[None, :] <= query_pos[:, None])
        return attention(query_rows, near_keys, near_values, allowed, HEADS)

    selected = lax.map(selected_branch, jnp.arange(SPAN // QBLOCK, dtype=jnp.int32)).reshape(SPAN, HEADS, DV)
    gate_values = jax.nn.sigmoid(gate_logits.astype(jnp.float32)).reshape(SPAN, 3, HEADS)
    combined = (gate_values[:, 0, :, None] * compressed + gate_values[:, 1, :, None] * selected
                + gate_values[:, 2, :, None] * sliding)
    return combined.reshape(SPAN, HEADS * DV).astype(jnp.bfloat16)
```

```python
import functools

import jax
import jax.numpy as jnp
from jax import lax
from jax.experimental import pallas as pl
from jax.experimental.pallas import tpu as pltpu
from jax.sharding import PartitionSpec as P

HEADS = 16
DK = 192
DV = 128
CMP_BLOCK = 32
SEL_BLOCK = 64
QBLOCK = 16
TOPN = 16
TOKENS = 128
NZ, NX = 16, 4
CHIPS = NZ * NX
DEVICES = 2 * CHIPS
PR, QR = 128, 224
VAL, HI, CMP = 0, 128, 192
WIN = 320
P_HALF = ((0, 64), (64, 128))
Q_HALF = ((0, 112), (112, 224))
MESH = pl.DeviceIdType.MESH
SCALE2 = DK**-0.5 * 1.4426950408889634
BF, F32 = jnp.bfloat16, jnp.float32
VMEM_LIMIT = 56 * 2**20


def pooled(rows, gains, mixing):
    summed = jnp.sum(rows.astype(F32).reshape(4, CMP_BLOCK, rows.shape[1]) * gains.astype(F32)[None], axis=1)
    return summed


def compressed(rows_of, gains, mixing):
    both = jnp.concatenate([pooled(rows_of[r], gains, mixing) for r in (0, 1)], axis=0)
    return jnp.dot(both.astype(BF), mixing, preferred_element_type=F32)


def paired_high(k):
    return jnp.concatenate([k[0:64, 128:192], k[64:128, 128:192]], axis=1)


def gather_kernel(keys, values, pos_k, pos_v, mix_k, mix_v, gp, gq, win, mine_p, mine_q, span,
                  pz, qz, px, qx, d2d, send, lsem, wrecv, wsend):
    me = lax.axis_index("ctx")
    z, x, c = me // 8, (me // 2) % 4, me % 2
    chip = me // 2

    def dev(zz, xx):
        return ((zz + NZ) % NZ) * 8 + ((xx + NX) % NX) * 2 + c

    def slot(zz, xx):
        return c * CHIPS + ((zz + 2 * NZ) % NZ) * NX + (xx + NX) % NX

    def zrow(zz):
        return pl.ds(c * CHIPS + ((zz + 2 * NZ) % NZ) * NX, NX)

    zn = [dev(z + 1, x), dev(z - 1, x)]
    xn = [dev(z, x + 1), dev(z, x - 1)]
    other = me + 1 - 2 * c

    def chip_dev(offset):
        return (chip + offset + CHIPS) % CHIPS * 2 + c

    near = [chip_dev(o) for o in (1, 2, -1, -2)]
    bar = pltpu.get_barrier_semaphore()
    for d in (*zn, *xn, other, *near):
        pl.semaphore_signal(bar, inc=1, device_id={"ctx": d}, device_id_type=MESH)

    mine_p[...] = keys[0, :, 0:128]
    mine_q[VAL : VAL + 128] = values[0]
    mine_q[HI : HI + 64] = paired_high(keys[0])
    ck = compressed(keys, pos_k[...], mix_k[...])
    cv = compressed(values, pos_v[...], mix_v[...])
    mine_q[CMP : CMP + 16] = jnp.concatenate([ck[:, 0:128], cv], axis=0).astype(BF)
    hi = jnp.concatenate([ck[:, 128:192], jnp.zeros((8, 64), F32)], axis=1)
    mine_q[CMP + 16 : CMP + 32] = jnp.concatenate([hi, jnp.zeros((8, 128), F32)], axis=0).astype(BF)
    for r in (0, 1):
        span[r, 0:128] = keys[r, :, 0:128]
        span[r, 128:256] = values[r]
        span[r, 256:320] = paired_high(keys[r])
    me_s = slot(z, x)
    local = [
        pltpu.make_async_copy(mine_p, gp.at[me_s], lsem.at[0]),
        pltpu.make_async_copy(mine_q, gq.at[me_s], lsem.at[1]),
        pltpu.make_async_copy(span.at[1], win.at[c], lsem.at[2]),
    ]
    for cp in local:
        cp.start()
    for cp in local:
        cp.wait()
    pl.semaphore_wait(bar, 9)

    def remote(ref, d, ss, rs, dst=None):
        return pltpu.make_async_remote_copy(
            src_ref=ref, dst_ref=ref if dst is None else dst, send_sem=ss, recv_sem=rs,
            device_id={"ctx": d}, device_id_type=MESH,
        )

    def part(buf, s, rows):
        return buf.at[s] if rows is None else buf.at[s, rows[0] : rows[1]]

    def sp(s, rows, d, rs):
        remote(part(gp, s, rows), d, send.at[0], rs).start()

    def sq(s, rows, d, rs):
        remote(part(gq, s, rows), d, send.at[1], rs).start()

    def wp(s, rows, rs):
        remote(part(gp, s, rows), other, send.at[0], rs).wait_recv()

    def wq(s, rows, rs):
        remote(part(gq, s, rows), other, send.at[1], rs).wait_recv()

    def zsend_p(zz, r, d, k, half):
        sp(slot(zz, x + r), P_HALF[d] if half else None, zn[d], pz.at[d, k, r])

    def zsend_q(zz, d, k, half):
        sq(slot(zz, x), Q_HALF[d] if half else None, zn[d], qz.at[d, k])

    def xsend_q(zz, t):
        for d in (0, 1):
            sq(slot(zz, x), None, xn[d], qx.at[t, d])

    def d2d_p(zz):
        remote(gp.at[zrow(zz)], other, send.at[2], d2d.at[0]).start()

    def d2d_q(zz):
        remote(gq.at[zrow(zz)], other, send.at[3], d2d.at[1]).start()

    for d in (0, 1):
        sp(me_s, None, xn[d], px.at[d])
    for d in (0, 1):
        zsend_q(z, d, 1, False)
    for d in (0, 1):
        zsend_p(z, 0, d, 1, False)
    xsend_q(z, 0)
    for o in (1, 2):
        wrapped = jnp.where(chip + o >= CHIPS, 0, 1)
        remote(span.at[wrapped], near[o - 1], wsend.at[o], wrecv.at[o], win.at[2 * o + c]).start()
    remote(win.at[c], other, wsend.at[0], wrecv.at[0]).start()
    for d, r in ((0, 3), (1, 1)):
        wp(slot(z, x + r), None, px.at[d])
        sp(slot(z, x + r), P_HALF[d], xn[d], px.at[2 + d])
        for e in (0, 1):
            zsend_p(z, r, e, 1, False)
    for d in (0, 1):
        wp(slot(z, x + 2), P_HALF[d], px.at[2 + d])
    for e in (0, 1):
        zsend_p(z, 2, e, 1, False)
    d2d_p(z)

    def qx_full(zz, t):
        for d, r in ((0, 3), (1, 1)):
            wq(slot(zz, x + r), None, qx.at[t, d])
            sq(slot(zz, x + r), Q_HALF[d], xn[d], qx.at[t, 2 + d])

    def qx_half(zz, t):
        for d in (0, 1):
            wq(slot(zz, x + 2), Q_HALF[d], qx.at[t, 2 + d])
        d2d_q(zz)

    def at_z(d, k):
        return z - k if d == 0 else z + k

    def at_t(d, k):
        return k if d == 0 else 8 + k

    def step(k, last):
        for d in (0, 1):
            wq(slot(at_z(d, k), x), None, qz.at[d, k])
            zsend_q(at_z(d, k), d, k + 1, last)
            xsend_q(at_z(d, k), at_t(d, k))
        for r in (0, 3, 1, 2):
            for d in (0, 1):
                wp(slot(at_z(d, k), x + r), None, pz.at[d, k, r])
                zsend_p(at_z(d, k), r, d, k + 1, last)
        for d in (0, 1):
            d2d_p(at_z(d, k))

    def lag1(k):
        for d in (0, 1):
            qx_full(at_z(d, k), at_t(d, k))

    def lag2(k):
        for d in (0, 1):
            qx_half(at_z(d, k), at_t(d, k))

    step(1, False)
    qx_full(z, 0)
    step(2, False)
    lag1(1)
    qx_half(z, 0)
    for o in (1, 2):
        remote(win.at[2 * o + c], other, wsend.at[o], wrecv.at[o]).wait_recv()
        remote(win.at[2 * o + c], other, wsend.at[2 + o], wrecv.at[2 + o]).start()

    def loop(k, carry):
        step(k, False)
        lag1(k - 1)
        lag2(k - 2)
        return carry

    lax.fori_loop(3, 7, loop, 0)
    step(7, True)
    lag1(6)
    lag2(5)
    for d in (0, 1):
        wq(slot(z - 8, x), Q_HALF[d], qz.at[d, 8])
    xsend_q(z - 8, 8)
    for r in (0, 3, 1, 2):
        for d in (0, 1):
            wp(slot(z - 8, x + r), P_HALF[d], pz.at[d, 8, r])
    d2d_p(z - 8)
    lag1(7)
    lag2(6)
    qx_full(z - 8, 8)
    lag2(7)
    qx_half(z - 8, 8)
    theirs = pl.ds((1 - c) * CHIPS, CHIPS)
    for n, buf in enumerate((gp, gq)):
        remote(buf.at[theirs], other, send.at[2 + n], d2d.at[n]).wait_recv()
    for o in (0, 1, 2):
        ref = win.at[2 * o + 1 - c]
        remote(ref, other, wsend.at[0], wrecv.at[o if o == 0 else 2 + o]).wait_recv()
    for n, buf in enumerate((gp, gq)):
        remote(buf.at[0 : CHIPS - 1], other, send.at[n], d2d.at[n]).wait_send()
        remote(buf.at[0:CHIPS], other, send.at[2 + n], d2d.at[n]).wait_send()
    for i in range(5):
        remote(win.at[0], other, wsend.at[i], wrecv.at[0]).wait_send()


def gather(keys, values, pos_k, pos_v, mix_k, mix_v):
    dma = pltpu.SemaphoreType.DMA
    shapes = [(DEVICES, PR, 128), (DEVICES, QR, 128), (6, WIN, 128)]
    return pl.pallas_call(
        gather_kernel,
        out_shape=[jax.ShapeDtypeStruct(s, BF) for s in shapes],
        in_specs=[pl.BlockSpec(memory_space=pltpu.VMEM)] * 6,
        out_specs=[pl.BlockSpec(memory_space=pl.ANY)] * 3,
        scratch_shapes=[
            pltpu.VMEM((PR, 128), BF),
            pltpu.VMEM((QR, 128), BF),
            pltpu.VMEM((2, WIN, 128), BF),
            dma((2, 9, 4)),
            dma((2, 9)),
            dma((4,)),
            dma((NZ, 4)),
            dma((2,)),
            dma((4,)),
            dma((3,)),
            dma((5,)),
            dma((5,)),
        ],
        compiler_params=pltpu.CompilerParams(
            collective_id=0, has_side_effects=True, vmem_limit_bytes=24 * 2**20
        ),
    )(keys, values, pos_k, pos_v, mix_k, mix_v)


def mixed(query_rows, key_rows, value_rows, bias):
    heads, tokens = query_rows.shape[0], query_rows.shape[1]
    count = key_rows.shape[0]
    scores = lax.dot_general(
        query_rows.reshape(heads * tokens, 256), key_rows, (((1,), (1,)), ((), ())), preferred_element_type=F32
    )
    scores = scores.reshape(heads, tokens, count) + bias[None]
    highest = jnp.max(scores, axis=2, keepdims=True)
    weights = jnp.exp2((scores - highest) * SCALE2).astype(BF)
    both = jnp.dot(weights.reshape(heads * tokens, count), value_rows, preferred_element_type=F32)
    return (both[:, 0:128] / both[:, 128:256]).reshape(heads, tokens, DV)


def prepare(q, gates, qs, gate_rows, vx):
    none = jnp.zeros((TOKENS, 64), BF)
    for h in range(HEADS):
        qs[h] = jnp.concatenate([q[:, h * DK : (h + 1) * DK], none], axis=1)
    g = jax.nn.sigmoid(gates[...].astype(F32))
    for i in range(3 * HEADS):
        gate_rows[i] = jnp.broadcast_to(g[:, i : i + 1], (TOKENS, DV))
    vx[:, 128:256] = jnp.ones((vx.shape[0], 128), BF)


def window_part(win, qs, gate_rows, acc, kx, vx, bias, c):
    for i in range(5):
        back = 4 - i - c
        off = (back + 1) // 2
        core = (2 * off - back) % 2
        piece = 2 * off + core
        rows = slice(128 * i, 128 * (i + 1))
        kx[rows, 0:128] = win[piece, 0:128]
        vx[rows, 0:128] = win[piece, 128:256]
        high = win[piece, 256:320]
        kx[128 * i : 128 * i + 64, 128:256] = high
        kx[128 * i + 64 : 128 * i + 128, 128:256] = pltpu.roll(high, 64, 1)
    count = 5 * TOKENS
    column = lax.broadcasted_iota(jnp.int32, (TOKENS, count), 1)
    token = lax.broadcasted_iota(jnp.int32, (TOKENS, count), 0)
    inside = (column > token) & (column <= 4 * TOKENS + token)
    bias[:, 0:count] = jnp.where(inside, 0.0, -jnp.inf)

    def heads(i, carry):
        at = pl.ds(2 * i, 2)
        o = mixed(qs[at], kx[0:count], vx[0:count], bias[:, 0:count])
        acc[at] = o * gate_rows[pl.ds(2 * HEADS + 2 * i, 2)]
        return carry

    lax.fori_loop(0, HEADS // 2, heads, 0)


def compressed_part(gq, qs, gate_rows, acc, kx, vx, bias, me):
    tile = gq[:, CMP : CMP + 16].astype(F32)
    count = DEVICES * 8
    kx[:, 0:128] = tile[:, 0:8].reshape(count, 128).astype(BF)
    vx[:, 0:128] = tile[:, 8:16].reshape(count, 128).astype(BF)
    kx[:, 128:256] = gq[:, CMP + 16 : CMP + 32].astype(F32)[:, 0:8].reshape(count, 128).astype(BF)
    column = lax.broadcasted_iota(jnp.int32, (TOKENS, count), 1)
    token = lax.broadcasted_iota(jnp.int32, (TOKENS, count), 0)
    where = column // 8
    holder = where % CHIPS * 2 + where // CHIPS
    within = column % 8
    end = jnp.where(within < 4, 0, (holder - me) * TOKENS + (within - 3) * CMP_BLOCK - 1)
    bias[...] = jnp.where(end <= token, 0.0, -jnp.inf)

    def heads(i, carry):
        at = pl.ds(2 * i, 2)
        o = mixed(qs[at], kx[...], vx[...], bias[...])
        acc[at] += o * gate_rows[at]
        return carry

    lax.fori_loop(0, HEADS // 2, heads, 0)


def selected_part(sel, gp, gq, win, qs, gate_rows, acc, kx, vx, out, c):
    count = TOPN * SEL_BLOCK

    def group(g, carry):
        mine = g // 4
        kx[0:64, 0:128] = win[c, pl.ds(pl.multiple_of(mine * 64, 64), 64)]
        vx[0:64, 0:128] = win[c, pl.ds(pl.multiple_of(128 + mine * 64, 64), 64)]
        high = win[c, 256:320]
        kx[0:64, 128:256] = jnp.where(mine == 1, pltpu.roll(high, 64, 1), high)
        for e in range(1, TOPN):
            block = jnp.maximum(sel[g, e], 0)
            piece, odd = block // 2, block % 2
            s = piece % 2 * CHIPS + piece // 2
            first = pl.multiple_of(odd * 64, 64)
            rows = slice(64 * e, 64 * (e + 1))
            kx[rows, 0:128] = gp[s, pl.ds(first, 64)]
            vx[rows, 0:128] = gq[s, pl.ds(first, 64)]
            high = gq[s, HI : HI + 64]
            kx[rows, 128:256] = jnp.where(odd == 1, pltpu.roll(high, 64, 1), high)
        column = lax.broadcasted_iota(jnp.int32, (QBLOCK, count), 1)
        token = lax.broadcasted_iota(jnp.int32, (QBLOCK, count), 0)
        bad = (column < SEL_BLOCK) & (column > (g % 4) * QBLOCK + token)
        for e in range(1, TOPN):
            bad = bad | ((column // SEL_BLOCK == e) & (sel[g, e] < 0))
        bias = jnp.where(bad, -jnp.inf, 0.0)
        rows = pl.ds(pl.multiple_of(g * QBLOCK, QBLOCK), QBLOCK)
        o = mixed(qs[:, rows], kx[...], vx[...], bias)
        o = acc[:, rows] + o * gate_rows[HEADS : 2 * HEADS, rows]
        for h in range(HEADS):
            out[rows, h * DV : (h + 1) * DV] = o[h].astype(BF)
        return carry

    lax.fori_loop(0, QBLOCK // 2, group, 0)


def attend_kernel(sel, q, gates, gp, gq, win, out, qs, gate_rows, acc, kx, vx, bias):
    me = lax.axis_index("ctx")
    c = me % 2
    prepare(q, gates, qs, gate_rows, vx)
    window_part(win, qs, gate_rows, acc, kx, vx, bias, c)
    compressed_part(gq, qs, gate_rows, acc, kx, vx, bias, me)
    selected_part(sel, gp, gq, win, qs, gate_rows, acc, kx, vx, out, c)


def attend(sel_ids, queries, gate_logits, gp, gq, win):
    vmem = pl.BlockSpec(memory_space=pltpu.VMEM)
    return pl.pallas_call(
        attend_kernel,
        out_shape=jax.ShapeDtypeStruct((TOKENS, HEADS * DV), BF),
        in_specs=[pl.BlockSpec(memory_space=pltpu.SMEM)] + [vmem] * 5,
        out_specs=vmem,
        scratch_shapes=[
            pltpu.VMEM((HEADS, TOKENS, 256), BF),
            pltpu.VMEM((3 * HEADS, TOKENS, DV), F32),
            pltpu.VMEM((HEADS, TOKENS, DV), F32),
            pltpu.VMEM((1024, 256), BF),
            pltpu.VMEM((1024, 256), BF),
            pltpu.VMEM((TOKENS, 1024), F32),
        ],
        compiler_params=pltpu.CompilerParams(vmem_limit_bytes=VMEM_LIMIT),
    )(sel_ids, queries, gate_logits, gp, gq, win)


def body(queries, keys, values, gate_logits, sel_ids, pos_k, pos_v, mix_k, mix_v):
    gp, gq, win = gather(keys, values, pos_k, pos_v, mix_k, mix_v)
    return attend(sel_ids, queries, gate_logits, gp, gq, win)


def solution(mesh):
    in_specs = (
        P("ctx", "grp"),
        P(None, "ctx", "grp"),
        P(None, "ctx", "grp"),
        P("ctx", "grp"),
        P("ctx", "grp"),
        P(None, "grp"),
        P(None, "grp"),
        P(None, "grp"),
        P(None, "grp"),
    )
    return jax.shard_map(body, mesh=mesh, in_specs=in_specs, out_specs=P("ctx", "grp"), check_vma=False)
```

```python
import functools

import jax
import jax.numpy as jnp
from jax import lax
from jax.experimental import pallas as pl
from jax.experimental.pallas import tpu as pltpu
from jax.sharding import PartitionSpec as P

HEADS = 16
DK = 192
DV = 128
CMP_BLOCK = 32
SEL_BLOCK = 64
QBLOCK = 16
TOPN = 16
TOKENS = 128
NZ, NX = 16, 4
CHIPS = NZ * NX
DEVICES = 2 * CHIPS
PR, QR = 128, 224
VAL, HI, CMP = 0, 128, 192
WIN = 320
P_HALF = ((0, 64), (64, 128))
Q_HALF = ((0, 112), (112, 224))
MESH = pl.DeviceIdType.MESH
SCALE2 = DK**-0.5 * 1.4426950408889634
BF, F32 = jnp.bfloat16, jnp.float32
VMEM_LIMIT = 56 * 2**20


def pooled(rows, gains, mixing):
    summed = jnp.sum(rows.astype(F32).reshape(4, CMP_BLOCK, rows.shape[1]) * gains.astype(F32)[None], axis=1)
    return summed


def compressed(rows_of, gains, mixing):
    both = jnp.concatenate([pooled(rows_of[r], gains, mixing) for r in (0, 1)], axis=0)
    return jnp.dot(both.astype(BF), mixing, preferred_element_type=F32)


def paired_high(k):
    return jnp.concatenate([k[0:64, 128:192], k[64:128, 128:192]], axis=1)


def fused_kernel(sel, q_in, keys_in, values_in, gates_in, pos_k_in, pos_v_in, mix_k_in, mix_v_in, out,
                 q, keys, values, gates, pos_k, pos_v, mix_k, mix_v,
                 gp, gq, win, span, qs, gate_rows, acc, kx, vx, bias,
                 pz, qz, px, qx, d2d, send, lsem, wrecv, wsend):
    me = lax.axis_index("ctx")
    z, x, c = me // 8, (me // 2) % 4, me % 2
    chip = me // 2

    def dev(zz, xx):
        return ((zz + NZ) % NZ) * 8 + ((xx + NX) % NX) * 2 + c

    def slot(zz, xx):
        return c * CHIPS + ((zz + 2 * NZ) % NZ) * NX + (xx + NX) % NX

    def zrow(zz):
        return pl.ds(c * CHIPS + ((zz + 2 * NZ) % NZ) * NX, NX)

    zn = [dev(z + 1, x), dev(z - 1, x)]
    xn = [dev(z, x + 1), dev(z, x - 1)]
    other = me + 1 - 2 * c

    def chip_dev(offset):
        return (chip + offset + CHIPS) % CHIPS * 2 + c

    near = [chip_dev(o) for o in (1, 2, -1, -2)]
    ins = (keys_in, values_in, pos_k_in, pos_v_in, mix_k_in, mix_v_in, gates_in, q_in)
    staged = (keys, values, pos_k, pos_v, mix_k, mix_v, gates, q)
    local = [pltpu.make_async_copy(r, v, lsem.at[i]) for i, (r, v) in enumerate(zip(ins, staged))]
    for cp in local:
        cp.start()
    bar = pltpu.get_barrier_semaphore()
    for d in (*zn, *xn, other, *near):
        pl.semaphore_signal(bar, inc=1, device_id={"ctx": d}, device_id_type=MESH)
    for cp in local[:6]:
        cp.wait()
    me_s = slot(z, x)
    rows = [keys[r].astype(F32).T.astype(BF) for r in (0, 1)]
    for r in (0, 1):
        span[r, 0:128] = rows[r][:, 0:128]
        span[r, 128:256] = values[r]
        span[r, 256:320] = paired_high(rows[r])
    gp[me_s] = span[0, 0:128]
    gq[me_s, VAL : VAL + 128] = values[0]
    gq[me_s, HI : HI + 64] = span[0, 256:320]
    ck = compressed(rows, pos_k[...], mix_k[...])
    cv = compressed(values, pos_v[...], mix_v[...])
    gq[me_s, CMP : CMP + 16] = jnp.concatenate([ck[:, 0:128], cv], axis=0).astype(BF)
    hi = jnp.concatenate([ck[:, 128:192], jnp.zeros((8, 64), F32)], axis=1)
    gq[me_s, CMP + 16 : CMP + 32] = jnp.concatenate([hi, jnp.zeros((8, 128), F32)], axis=0).astype(BF)
    win[c] = span[1]
    pl.semaphore_wait(bar, 9)

    def remote(ref, d, ss, rs, dst=None):
        return pltpu.make_async_remote_copy(
            src_ref=ref, dst_ref=ref if dst is None else dst, send_sem=ss, recv_sem=rs,
            device_id={"ctx": d}, device_id_type=MESH,
        )

    def part(buf, s, rows):
        return buf.at[s] if rows is None else buf.at[s, rows[0] : rows[1]]

    def sp(s, rows, d, rs):
        remote(part(gp, s, rows), d, send.at[0], rs).start()

    def sq(s, rows, d, rs):
        remote(part(gq, s, rows), d, send.at[1], rs).start()

    def wp(s, rows, rs):
        remote(part(gp, s, rows), other, send.at[0], rs).wait_recv()

    def wq(s, rows, rs):
        remote(part(gq, s, rows), other, send.at[1], rs).wait_recv()

    def zsend_p(zz, r, d, k, half):
        sp(slot(zz, x + r), P_HALF[d] if half else None, zn[d], pz.at[d, k, r])

    def zsend_q(zz, d, k, half):
        sq(slot(zz, x), Q_HALF[d] if half else None, zn[d], qz.at[d, k])

    def xsend_q(zz, t):
        for d in (0, 1):
            sq(slot(zz, x), None, xn[d], qx.at[t, d])

    def d2d_p(zz):
        remote(gp.at[zrow(zz)], other, send.at[2], d2d.at[0]).start()

    def d2d_q(zz):
        remote(gq.at[zrow(zz)], other, send.at[3], d2d.at[1]).start()

    for d in (0, 1):
        sp(me_s, None, xn[d], px.at[d])
    for d in (0, 1):
        zsend_q(z, d, 1, False)
    for d in (0, 1):
        zsend_p(z, 0, d, 1, False)
    xsend_q(z, 0)
    for o in (1, 2):
        wrapped = jnp.where(chip + o >= CHIPS, 0, 1)
        remote(span.at[wrapped], near[o - 1], wsend.at[o], wrecv.at[o], win.at[2 * o + c]).start()
    remote(win.at[c], other, wsend.at[0], wrecv.at[0]).start()
    for d, r in ((0, 3), (1, 1)):
        wp(slot(z, x + r), None, px.at[d])
        sp(slot(z, x + r), P_HALF[d], xn[d], px.at[2 + d])
        for e in (0, 1):
            zsend_p(z, r, e, 1, False)
    for d in (0, 1):
        wp(slot(z, x + 2), P_HALF[d], px.at[2 + d])
    for e in (0, 1):
        zsend_p(z, 2, e, 1, False)
    d2d_p(z)
    for cp in local[6:]:
        cp.wait()
    prepare(q, gates, qs, gate_rows, vx)

    def qx_full(zz, t):
        for d, r in ((0, 3), (1, 1)):
            wq(slot(zz, x + r), None, qx.at[t, d])
            sq(slot(zz, x + r), Q_HALF[d], xn[d], qx.at[t, 2 + d])

    def qx_half(zz, t):
        for d in (0, 1):
            wq(slot(zz, x + 2), Q_HALF[d], qx.at[t, 2 + d])
        d2d_q(zz)

    def at_z(d, k):
        return z - k if d == 0 else z + k

    def at_t(d, k):
        return k if d == 0 else 8 + k

    def step(k, last):
        for d in (0, 1):
            wq(slot(at_z(d, k), x), None, qz.at[d, k])
            zsend_q(at_z(d, k), d, k + 1, last)
            xsend_q(at_z(d, k), at_t(d, k))
        for r in (0, 3, 1, 2):
            for d in (0, 1):
                wp(slot(at_z(d, k), x + r), None, pz.at[d, k, r])
                zsend_p(at_z(d, k), r, d, k + 1, last)
        for d in (0, 1):
            d2d_p(at_z(d, k))

    def lag1(k):
        for d in (0, 1):
            qx_full(at_z(d, k), at_t(d, k))

    def lag2(k):
        for d in (0, 1):
            qx_half(at_z(d, k), at_t(d, k))

    step(1, False)
    qx_full(z, 0)
    step(2, False)
    lag1(1)
    qx_half(z, 0)
    for o in (1, 2):
        remote(win.at[2 * o + c], other, wsend.at[o], wrecv.at[o]).wait_recv()
        remote(win.at[2 * o + c], other, wsend.at[2 + o], wrecv.at[2 + o]).start()

    for o in (0, 1, 2):
        ref = win.at[2 * o + 1 - c]
        remote(ref, other, wsend.at[0], wrecv.at[o if o == 0 else 2 + o]).wait_recv()
    window_keys(win, kx, vx, bias, c)

    def loop(k, carry):
        step(k, False)
        window_heads(2 * (k - 3), qs, gate_rows, acc, kx, vx, bias)
        lag1(k - 1)
        window_heads(2 * (k - 3) + 1, qs, gate_rows, acc, kx, vx, bias)
        lag2(k - 2)
        return carry

    lax.fori_loop(3, 7, loop, 0)
    step(7, True)
    lag1(6)
    lag2(5)
    for d in (0, 1):
        wq(slot(z - 8, x), Q_HALF[d], qz.at[d, 8])
    xsend_q(z - 8, 8)
    for r in (0, 3, 1, 2):
        for d in (0, 1):
            wp(slot(z - 8, x + r), P_HALF[d], pz.at[d, 8, r])
    d2d_p(z - 8)
    lag1(7)
    lag2(6)
    qx_full(z - 8, 8)
    lag2(7)
    qx_half(z - 8, 8)
    theirs = pl.ds((1 - c) * CHIPS, CHIPS)
    for n, buf in enumerate((gp, gq)):
        remote(buf.at[theirs], other, send.at[2 + n], d2d.at[n]).wait_recv()
    compressed_part(gq, qs, gate_rows, acc, kx, vx, bias, me)
    selected_part(sel, gp, gq, win, qs, gate_rows, acc, kx, vx, out, c)
    for n, buf in enumerate((gp, gq)):
        remote(buf.at[0 : CHIPS - 1], other, send.at[n], d2d.at[n]).wait_send()
        remote(buf.at[0:CHIPS], other, send.at[2 + n], d2d.at[n]).wait_send()
    for i in range(5):
        remote(win.at[0], other, wsend.at[i], wrecv.at[0]).wait_send()


def mixed(query_rows, key_rows, value_rows, bias):
    heads, tokens = query_rows.shape[0], query_rows.shape[1]
    count = key_rows.shape[0]
    scores = lax.dot_general(
        query_rows.reshape(heads * tokens, 256), key_rows, (((1,), (1,)), ((), ())), preferred_element_type=F32
    )
    scores = scores.reshape(heads, tokens, count) + bias[None]
    highest = jnp.max(scores, axis=2, keepdims=True)
    weights = jnp.exp2((scores - highest) * SCALE2).astype(BF)
    both = jnp.dot(weights.reshape(heads * tokens, count), value_rows, preferred_element_type=F32)
    return (both[:, 0:128] / both[:, 128:256]).reshape(heads, tokens, DV)


def prepare(q, gates, qs, gate_rows, vx):
    none = jnp.zeros((TOKENS, 64), BF)
    for h in range(HEADS):
        qs[h] = jnp.concatenate([q[:, h * DK : (h + 1) * DK], none], axis=1)
    g = jax.nn.sigmoid(gates[...].astype(F32)).T
    for i in range(3 * HEADS):
        gate_rows[i] = jnp.broadcast_to(g[:, i : i + 1], (TOKENS, DV))
    vx[:, 128:256] = jnp.ones((vx.shape[0], 128), BF)


def window_keys(win, kx, vx, bias, c):
    for i in range(5):
        back = 4 - i - c
        off = (back + 1) // 2
        core = (2 * off - back) % 2
        piece = 2 * off + core
        rows = slice(128 * i, 128 * (i + 1))
        kx[rows, 0:128] = win[piece, 0:128]
        vx[rows, 0:128] = win[piece, 128:256]
        high = win[piece, 256:320]
        kx[128 * i : 128 * i + 64, 128:256] = high
        kx[128 * i + 64 : 128 * i + 128, 128:256] = pltpu.roll(high, 64, 1)
    count = 5 * TOKENS
    column = lax.broadcasted_iota(jnp.int32, (TOKENS, count), 1)
    token = lax.broadcasted_iota(jnp.int32, (TOKENS, count), 0)
    inside = (column > token) & (column <= 4 * TOKENS + token)
    bias[:, 0:count] = jnp.where(inside, 0.0, -jnp.inf)


def window_heads(i, qs, gate_rows, acc, kx, vx, bias):
    count = 5 * TOKENS
    at = pl.ds(2 * i, 2)
    o = mixed(qs[at], kx[0:count], vx[0:count], bias[:, 0:count])
    acc[at] = o * gate_rows[pl.ds(2 * HEADS + 2 * i, 2)]


def compressed_part(gq, qs, gate_rows, acc, kx, vx, bias, me):
    tile = gq[:, CMP : CMP + 16].astype(F32)
    count = DEVICES * 8
    kx[:, 0:128] = tile[:, 0:8].reshape(count, 128).astype(BF)
    vx[:, 0:128] = tile[:, 8:16].reshape(count, 128).astype(BF)
    kx[:, 128:256] = gq[:, CMP + 16 : CMP + 32].astype(F32)[:, 0:8].reshape(count, 128).astype(BF)
    column = lax.broadcasted_iota(jnp.int32, (TOKENS, count), 1)
    token = lax.broadcasted_iota(jnp.int32, (TOKENS, count), 0)
    where = column // 8
    holder = where % CHIPS * 2 + where // CHIPS
    within = column % 8
    end = jnp.where(within < 4, 0, (holder - me) * TOKENS + (within - 3) * CMP_BLOCK - 1)
    bias[...] = jnp.where(end <= token, 0.0, -jnp.inf)

    def heads(i, carry):
        at = pl.ds(2 * i, 2)
        o = mixed(qs[at], kx[...], vx[...], bias[...])
        acc[at] += o * gate_rows[at]
        return carry

    lax.fori_loop(0, HEADS // 2, heads, 0)


def selected_part(sel, gp, gq, win, qs, gate_rows, acc, kx, vx, out, c):
    count = TOPN * SEL_BLOCK

    def group(g, carry):
        mine = g // 4
        kx[0:64, 0:128] = win[c, pl.ds(pl.multiple_of(mine * 64, 64), 64)]
        vx[0:64, 0:128] = win[c, pl.ds(pl.multiple_of(128 + mine * 64, 64), 64)]
        high = win[c, 256:320]
        kx[0:64, 128:256] = jnp.where(mine == 1, pltpu.roll(high, 64, 1), high)
        for e in range(1, TOPN):
            block = jnp.maximum(sel[g, e], 0)
            odd = block & 1
            s = ((block >> 1) & 1) * CHIPS + (block >> 2)
            second = jnp.broadcast_to(odd, (64, 128)) == 1
            low, rest = gp[s], gq[s]
            high = rest[HI : HI + 64]
            rows = slice(64 * e, 64 * (e + 1))
            kx[rows, 0:128] = jnp.where(second, low[64:128], low[0:64])
            vx[rows, 0:128] = jnp.where(second, rest[64:128], rest[0:64])
            kx[rows, 128:256] = jnp.where(second, pltpu.roll(high, 64, 1), high)
        column = lax.broadcasted_iota(jnp.int32, (QBLOCK, count), 1)
        token = lax.broadcasted_iota(jnp.int32, (QBLOCK, count), 0)
        bad = (column < SEL_BLOCK) & (column > (g % 4) * QBLOCK + token)
        for e in range(1, TOPN):
            bad = bad | ((column // SEL_BLOCK == e) & (jnp.broadcast_to(sel[g, e], (QBLOCK, count)) < 0))
        bias = jnp.where(bad, -jnp.inf, 0.0)
        rows = pl.ds(pl.multiple_of(g * QBLOCK, QBLOCK), QBLOCK)
        o = mixed(qs[:, rows], kx[...], vx[...], bias)
        o = acc[:, rows] + o * gate_rows[HEADS : 2 * HEADS, rows]
        for h in range(HEADS):
            out[rows, h * DV : (h + 1) * DV] = o[h].astype(BF)
        return carry

    lax.fori_loop(0, QBLOCK // 2, group, 0)


def body(queries, keys, values, gate_logits, sel_ids, pos_k, pos_v, mix_k, mix_v):
    dma = pltpu.SemaphoreType.DMA
    turned = (
        queries, keys.transpose(0, 2, 1), values, gate_logits.transpose(1, 0), pos_k, pos_v, mix_k, mix_v
    )
    anywhere = pl.BlockSpec(memory_space=pl.ANY)
    return pl.pallas_call(
        fused_kernel,
        out_shape=jax.ShapeDtypeStruct((TOKENS, HEADS * DV), BF),
        in_specs=[pl.BlockSpec(memory_space=pltpu.SMEM)] + [anywhere] * 8,
        out_specs=pl.BlockSpec(memory_space=pltpu.VMEM),
        scratch_shapes=[
            *(pltpu.VMEM(a.shape, BF) for a in turned),
            pltpu.VMEM((DEVICES, PR, 128), BF),
            pltpu.VMEM((DEVICES, QR, 128), BF),
            pltpu.VMEM((6, WIN, 128), BF),
            pltpu.VMEM((2, WIN, 128), BF),
            pltpu.VMEM((HEADS, TOKENS, 256), BF),
            pltpu.VMEM((3 * HEADS, TOKENS, DV), F32),
            pltpu.VMEM((HEADS, TOKENS, DV), F32),
            pltpu.VMEM((1024, 256), BF),
            pltpu.VMEM((1024, 256), BF),
            pltpu.VMEM((TOKENS, 1024), F32),
            dma((2, 9, 4)),
            dma((2, 9)),
            dma((4,)),
            dma((NZ, 4)),
            dma((2,)),
            dma((4,)),
            dma((8,)),
            dma((5,)),
            dma((5,)),
        ],
        compiler_params=pltpu.CompilerParams(
            collective_id=0, has_side_effects=True, vmem_limit_bytes=VMEM_LIMIT
        ),
    )(sel_ids, *turned)


def solution(mesh):
    in_specs = (
        P("ctx", "grp"),
        P(None, "ctx", "grp"),
        P(None, "ctx", "grp"),
        P("ctx", "grp"),
        P("ctx", "grp"),
        P(None, "grp"),
        P(None, "grp"),
        P(None, "grp"),
        P(None, "grp"),
    )
    return jax.shard_map(body, mesh=mesh, in_specs=in_specs, out_specs=P("ctx", "grp"), check_vma=False)
```

```python
import functools

import jax
import jax.numpy as jnp
from jax import lax
from jax.experimental import pallas as pl
from jax.experimental.pallas import tpu as pltpu
from jax.sharding import PartitionSpec as P

HEADS = 16
DK = 192
DV = 128
CMP_BLOCK = 32
SEL_BLOCK = 64
QBLOCK = 16
TOPN = 16
TOKENS = 128
NZ, NX = 16, 4
CHIPS = NZ * NX
DEVICES = 2 * CHIPS
PR, QR = 128, 224
VAL, HI, CMP = 0, 128, 192
WIN = 320
P_HALF = ((0, 64), (64, 128))
Q_HALF = ((0, 112), (112, 224))
MESH = pl.DeviceIdType.MESH
SCALE2 = DK**-0.5 * 1.4426950408889634
BF, F32 = jnp.bfloat16, jnp.float32
VMEM_LIMIT = 56 * 2**20


def pooled(rows, gains, mixing):
    summed = jnp.sum(rows.astype(F32).reshape(4, CMP_BLOCK, rows.shape[1]) * gains.astype(F32)[None], axis=1)
    return summed


def compressed(rows_of, gains, mixing):
    both = jnp.concatenate([pooled(rows_of[r], gains, mixing) for r in (0, 1)], axis=0)
    return jnp.dot(both.astype(BF), mixing, preferred_element_type=F32)


def paired_high(k):
    return jnp.concatenate([k[0:64, 128:192], k[64:128, 128:192]], axis=1)


def fused_kernel(sel, q_in, keys_in, values_in, gates_in, pos_k_in, pos_v_in, mix_k_in, mix_v_in, out,
                 q, keys, values, gates, pos_k, pos_v, mix_k, mix_v,
                 gp, gq, win, span, qs, gate_rows, acc, kx, vx, bias,
                 pz, qz, px, qx, d2d, send, lsem, wrecv, wsend):
    me = lax.axis_index("ctx")
    z, x, c = me // 8, (me // 2) % 4, me % 2
    chip = me // 2

    def dev(zz, xx):
        return ((zz + NZ) % NZ) * 8 + ((xx + NX) % NX) * 2 + c

    def slot(zz, xx):
        return c * CHIPS + ((zz + 2 * NZ) % NZ) * NX + (xx + NX) % NX

    def zrow(zz):
        return pl.ds(c * CHIPS + ((zz + 2 * NZ) % NZ) * NX, NX)

    zn = [dev(z + 1, x), dev(z - 1, x)]
    xn = [dev(z, x + 1), dev(z, x - 1)]
    other = me + 1 - 2 * c

    def chip_dev(offset):
        return (chip + offset + CHIPS) % CHIPS * 2 + c

    near = [chip_dev(o) for o in (1, 2, -1, -2)]
    ins = (keys_in, values_in, pos_k_in, pos_v_in, mix_k_in, mix_v_in, gates_in, q_in)
    staged = (keys, values, pos_k, pos_v, mix_k, mix_v, gates, q)
    local = [pltpu.make_async_copy(r, v, lsem.at[i]) for i, (r, v) in enumerate(zip(ins, staged))]
    for cp in local:
        cp.start()
    bar = pltpu.get_barrier_semaphore()
    for d in (*zn, *xn, other, *near):
        pl.semaphore_signal(bar, inc=1, device_id={"ctx": d}, device_id_type=MESH)
    for cp in local[:6]:
        cp.wait()
    me_s = slot(z, x)
    rows = [keys[r].astype(F32).T.astype(BF) for r in (0, 1)]
    for r in (0, 1):
        span[r, 0:128] = rows[r][:, 0:128]
        span[r, 128:256] = values[r]
        span[r, 256:320] = paired_high(rows[r])
    gp[me_s] = span[0, 0:128]
    gq[me_s, VAL : VAL + 128] = values[0]
    gq[me_s, HI : HI + 64] = span[0, 256:320]
    ck = compressed(rows, pos_k[...], mix_k[...])
    cv = compressed(values, pos_v[...], mix_v[...])
    gq[me_s, CMP : CMP + 16] = jnp.concatenate([ck[:, 0:128], cv], axis=0).astype(BF)
    hi = jnp.concatenate([ck[:, 128:192], jnp.zeros((8, 64), F32)], axis=1)
    gq[me_s, CMP + 16 : CMP + 32] = jnp.concatenate([hi, jnp.zeros((8, 128), F32)], axis=0).astype(BF)
    win[c] = span[1]
    pl.semaphore_wait(bar, 9)

    def remote(ref, d, ss, rs, dst=None):
        return pltpu.make_async_remote_copy(
            src_ref=ref, dst_ref=ref if dst is None else dst, send_sem=ss, recv_sem=rs,
            device_id={"ctx": d}, device_id_type=MESH,
        )

    def part(buf, s, rows):
        return buf.at[s] if rows is None else buf.at[s, rows[0] : rows[1]]

    def sp(s, rows, d, rs):
        remote(part(gp, s, rows), d, send.at[0], rs).start()

    def sq(s, rows, d, rs):
        remote(part(gq, s, rows), d, send.at[1], rs).start()

    def wp(s, rows, rs):
        remote(part(gp, s, rows), other, send.at[0], rs).wait_recv()

    def wq(s, rows, rs):
        remote(part(gq, s, rows), other, send.at[1], rs).wait_recv()

    def zsend_p(zz, r, d, k, half):
        sp(slot(zz, x + r), P_HALF[d] if half else None, zn[d], pz.at[d, k, r])

    def zsend_q(zz, d, k, half):
        sq(slot(zz, x), Q_HALF[d] if half else None, zn[d], qz.at[d, k])

    def xsend_q(zz, t):
        for d in (0, 1):
            sq(slot(zz, x), None, xn[d], qx.at[t, d])

    def d2d_p(zz):
        remote(gp.at[zrow(zz)], other, send.at[2], d2d.at[0]).start()

    def d2d_q(zz):
        remote(gq.at[zrow(zz)], other, send.at[3], d2d.at[1]).start()

    for d in (0, 1):
        sp(me_s, None, xn[d], px.at[d])
    for d in (0, 1):
        zsend_q(z, d, 1, False)
    for d in (0, 1):
        zsend_p(z, 0, d, 1, False)
    xsend_q(z, 0)
    for o in (1, 2):
        wrapped = jnp.where(chip + o >= CHIPS, 0, 1)
        remote(span.at[wrapped], near[o - 1], wsend.at[o], wrecv.at[o], win.at[2 * o + c]).start()
    remote(win.at[c], other, wsend.at[0], wrecv.at[0]).start()
    for d, r in ((0, 3), (1, 1)):
        wp(slot(z, x + r), None, px.at[d])
        sp(slot(z, x + r), P_HALF[d], xn[d], px.at[2 + d])
        for e in (0, 1):
            zsend_p(z, r, e, 1, False)
    for d in (0, 1):
        wp(slot(z, x + 2), P_HALF[d], px.at[2 + d])
    for e in (0, 1):
        zsend_p(z, 2, e, 1, False)
    d2d_p(z)
    for cp in local[6:]:
        cp.wait()
    prepare(q, gates, qs, gate_rows, vx)

    def qx_full(zz, t):
        for d, r in ((0, 3), (1, 1)):
            wq(slot(zz, x + r), None, qx.at[t, d])
            sq(slot(zz, x + r), Q_HALF[d], xn[d], qx.at[t, 2 + d])

    def qx_half(zz, t):
        for d in (0, 1):
            wq(slot(zz, x + 2), Q_HALF[d], qx.at[t, 2 + d])
        d2d_q(zz)

    def at_z(d, k):
        return z - k if d == 0 else z + k

    def at_t(d, k):
        return k if d == 0 else 8 + k

    def step(k, last):
        for d in (0, 1):
            wq(slot(at_z(d, k), x), None, qz.at[d, k])
            zsend_q(at_z(d, k), d, k + 1, last)
            xsend_q(at_z(d, k), at_t(d, k))
        for r in (0, 3, 1, 2):
            for d in (0, 1):
                wp(slot(at_z(d, k), x + r), None, pz.at[d, k, r])
                zsend_p(at_z(d, k), r, d, k + 1, last)
        for d in (0, 1):
            d2d_p(at_z(d, k))

    def lag1(k):
        for d in (0, 1):
            qx_full(at_z(d, k), at_t(d, k))

    def lag2(k):
        for d in (0, 1):
            qx_half(at_z(d, k), at_t(d, k))

    step(1, False)
    qx_full(z, 0)
    step(2, False)
    lag1(1)
    qx_half(z, 0)
    for o in (1, 2):
        remote(win.at[2 * o + c], other, wsend.at[o], wrecv.at[o]).wait_recv()
        remote(win.at[2 * o + c], other, wsend.at[2 + o], wrecv.at[2 + o]).start()

    for o in (0, 1, 2):
        ref = win.at[2 * o + 1 - c]
        remote(ref, other, wsend.at[0], wrecv.at[o if o == 0 else 2 + o]).wait_recv()
    window_keys(win, kx.at[0], vx.at[0], bias, c)

    def loop(k, carry):
        step(k, False)
        for i in (0, 1):
            window_heads(2 * (k - 3) + i, qs, gate_rows, acc, kx.at[0], vx.at[0], bias)
        lag1(k - 1)
        lag2(k - 2)
        return carry

    lax.fori_loop(3, 7, loop, 0)
    step(7, True)
    lag1(6)
    lag2(5)
    for d in (0, 1):
        wq(slot(z - 8, x), Q_HALF[d], qz.at[d, 8])
    xsend_q(z - 8, 8)
    for r in (0, 3, 1, 2):
        for d in (0, 1):
            wp(slot(z - 8, x + r), P_HALF[d], pz.at[d, 8, r])
    d2d_p(z - 8)
    lag1(7)
    lag2(6)
    qx_full(z - 8, 8)
    lag2(7)
    qx_half(z - 8, 8)
    theirs = pl.ds((1 - c) * CHIPS, CHIPS)
    for n, buf in enumerate((gp, gq)):
        remote(buf.at[theirs], other, send.at[2 + n], d2d.at[n]).wait_recv()
    compressed_part(gq, qs, gate_rows, acc, kx.at[1], vx.at[1], bias, me)
    selected_part(sel, gp, gq, win, qs, gate_rows, acc, kx, vx, out, c)
    for n, buf in enumerate((gp, gq)):
        remote(buf.at[0 : CHIPS - 1], other, send.at[n], d2d.at[n]).wait_send()
        remote(buf.at[0:CHIPS], other, send.at[2 + n], d2d.at[n]).wait_send()
    for i in range(5):
        remote(win.at[0], other, wsend.at[i], wrecv.at[0]).wait_send()


def mixed(query_rows, key_rows, value_rows, bias):
    heads, tokens = query_rows.shape[0], query_rows.shape[1]
    count = key_rows.shape[0]
    scores = lax.dot_general(
        query_rows.reshape(heads * tokens, 256), key_rows, (((1,), (1,)), ((), ())), preferred_element_type=F32
    )
    scores = scores.reshape(heads, tokens, count) + bias[None]
    highest = jnp.max(scores, axis=2, keepdims=True)
    weights = jnp.exp2((scores - highest) * SCALE2).astype(BF)
    both = jnp.dot(weights.reshape(heads * tokens, count), value_rows, preferred_element_type=F32)
    return (both[:, 0:128] / both[:, 128:256]).reshape(heads, tokens, DV)


def prepare(q, gates, qs, gate_rows, vx):
    none = jnp.zeros((TOKENS, 64), BF)
    for h in range(HEADS):
        qs[h] = jnp.concatenate([q[:, h * DK : (h + 1) * DK], none], axis=1)
    g = jax.nn.sigmoid(gates[...].astype(F32)).T
    for i in range(3 * HEADS):
        gate_rows[i] = jnp.broadcast_to(g[:, i : i + 1], (TOKENS, DV))
    vx[:, :, 128:256] = jnp.ones((2, vx.shape[1], 128), BF)


def window_keys(win, kx, vx, bias, c):
    for i in range(5):
        back = 4 - i - c
        off = (back + 1) // 2
        core = (2 * off - back) % 2
        piece = 2 * off + core
        rows = slice(128 * i, 128 * (i + 1))
        kx[rows, 0:128] = win[piece, 0:128]
        vx[rows, 0:128] = win[piece, 128:256]
        high = win[piece, 256:320]
        kx[128 * i : 128 * i + 64, 128:256] = high
        kx[128 * i + 64 : 128 * i + 128, 128:256] = pltpu.roll(high, 64, 1)
    count = 5 * TOKENS
    column = lax.broadcasted_iota(jnp.int32, (TOKENS, count), 1)
    token = lax.broadcasted_iota(jnp.int32, (TOKENS, count), 0)
    inside = (column > token) & (column <= 4 * TOKENS + token)
    bias[:, 0:count] = jnp.where(inside, 0.0, -jnp.inf)


def window_heads(i, qs, gate_rows, acc, kx, vx, bias):
    count = 5 * TOKENS
    at = pl.ds(2 * i, 2)
    o = mixed(qs[at], kx[0:count], vx[0:count], bias[:, 0:count])
    acc[at] = o * gate_rows[pl.ds(2 * HEADS + 2 * i, 2)]


def compressed_part(gq, qs, gate_rows, acc, kx, vx, bias, me):
    tile = gq[:, CMP : CMP + 16].astype(F32)
    count = DEVICES * 8
    kx[:, 0:128] = tile[:, 0:8].reshape(count, 128).astype(BF)
    vx[:, 0:128] = tile[:, 8:16].reshape(count, 128).astype(BF)
    kx[:, 128:256] = gq[:, CMP + 16 : CMP + 32].astype(F32)[:, 0:8].reshape(count, 128).astype(BF)
    column = lax.broadcasted_iota(jnp.int32, (TOKENS, count), 1)
    token = lax.broadcasted_iota(jnp.int32, (TOKENS, count), 0)
    where = column // 8
    holder = where % CHIPS * 2 + where // CHIPS
    within = column % 8
    end = jnp.where(within < 4, 0, (holder - me) * TOKENS + (within - 3) * CMP_BLOCK - 1)
    bias[...] = jnp.where(end <= token, 0.0, -jnp.inf)

    def heads(i, carry):
        at = pl.ds(2 * i, 2)
        o = mixed(qs[at], kx[...], vx[...], bias[...])
        acc[at] += o * gate_rows[at]
        return carry

    lax.fori_loop(0, HEADS // 2, heads, 0, unroll=True)


def selected_part(sel, gp, gq, win, qs, gate_rows, acc, key_slots, value_slots, out, c):
    count = TOPN * SEL_BLOCK

    def group(g, carry):
        mine = g // 4
        kx, vx = key_slots.at[g % 2], value_slots.at[g % 2]
        kx[0:64, 0:128] = win[c, pl.ds(pl.multiple_of(mine * 64, 64), 64)]
        vx[0:64, 0:128] = win[c, pl.ds(pl.multiple_of(128 + mine * 64, 64), 64)]
        high = win[c, 256:320]
        kx[0:64, 128:256] = jnp.where(mine == 1, pltpu.roll(high, 64, 1), high)
        for e in range(1, TOPN):
            block = jnp.maximum(sel[g, e], 0)
            odd = block & 1
            s = ((block >> 1) & 1) * CHIPS + (block >> 2)
            second = jnp.broadcast_to(odd, (64, 128)) == 1
            low, rest = gp[s], gq[s]
            high = rest[HI : HI + 64]
            rows = slice(64 * e, 64 * (e + 1))
            kx[rows, 0:128] = jnp.where(second, low[64:128], low[0:64])
            vx[rows, 0:128] = jnp.where(second, rest[64:128], rest[0:64])
            kx[rows, 128:256] = jnp.where(second, pltpu.roll(high, 64, 1), high)
        column = lax.broadcasted_iota(jnp.int32, (QBLOCK, count), 1)
        token = lax.broadcasted_iota(jnp.int32, (QBLOCK, count), 0)
        bad = (column < SEL_BLOCK) & (column > (g % 4) * QBLOCK + token)
        for e in range(1, TOPN):
            bad = bad | ((column // SEL_BLOCK == e) & (jnp.broadcast_to(sel[g, e], (QBLOCK, count)) < 0))
        bias = jnp.where(bad, -jnp.inf, 0.0)
        rows = pl.ds(pl.multiple_of(g * QBLOCK, QBLOCK), QBLOCK)
        o = mixed(qs[:, rows], kx[...], vx[...], bias)
        o = acc[:, rows] + o * gate_rows[HEADS : 2 * HEADS, rows]
        for h in range(HEADS):
            out[rows, h * DV : (h + 1) * DV] = o[h].astype(BF)
        return carry

    lax.fori_loop(0, QBLOCK // 2, group, 0, unroll=True)


def body(queries, keys, values, gate_logits, sel_ids, pos_k, pos_v, mix_k, mix_v):
    dma = pltpu.SemaphoreType.DMA
    turned = (
        queries, keys.transpose(0, 2, 1), values, gate_logits.transpose(1, 0), pos_k, pos_v, mix_k, mix_v
    )
    anywhere = pl.BlockSpec(memory_space=pl.ANY)
    return pl.pallas_call(
        fused_kernel,
        out_shape=jax.ShapeDtypeStruct((TOKENS, HEADS * DV), BF),
        in_specs=[pl.BlockSpec(memory_space=pltpu.SMEM)] + [anywhere] * 8,
        out_specs=pl.BlockSpec(memory_space=pltpu.VMEM),
        scratch_shapes=[
            *(pltpu.VMEM(a.shape, BF) for a in turned),
            pltpu.VMEM((DEVICES, PR, 128), BF),
            pltpu.VMEM((DEVICES, QR, 128), BF),
            pltpu.VMEM((6, WIN, 128), BF),
            pltpu.VMEM((2, WIN, 128), BF),
            pltpu.VMEM((HEADS, TOKENS, 256), BF),
            pltpu.VMEM((3 * HEADS, TOKENS, DV), F32),
            pltpu.VMEM((HEADS, TOKENS, DV), F32),
            pltpu.VMEM((2, 1024, 256), BF),
            pltpu.VMEM((2, 1024, 256), BF),
            pltpu.VMEM((TOKENS, 1024), F32),
            dma((2, 9, 4)),
            dma((2, 9)),
            dma((4,)),
            dma((NZ, 4)),
            dma((2,)),
            dma((4,)),
            dma((8,)),
            dma((5,)),
            dma((5,)),
        ],
        compiler_params=pltpu.CompilerParams(
            collective_id=0, has_side_effects=True, vmem_limit_bytes=VMEM_LIMIT
        ),
    )(sel_ids, *turned)


def solution(mesh):
    in_specs = (
        P("ctx", "grp"),
        P(None, "ctx", "grp"),
        P(None, "ctx", "grp"),
        P("ctx", "grp"),
        P("ctx", "grp"),
        P(None, "grp"),
        P(None, "grp"),
        P(None, "grp"),
        P(None, "grp"),
    )
    return jax.shard_map(body, mesh=mesh, in_specs=in_specs, out_specs=P("ctx", "grp"), check_vma=False)
```

```python
import functools

import jax
import jax.numpy as jnp
from jax import lax
from jax.experimental import pallas as pl
from jax.experimental.pallas import tpu as pltpu
from jax.sharding import PartitionSpec as P

HEADS = 16
DK = 192
DV = 128
CMP_BLOCK = 32
SEL_BLOCK = 64
QBLOCK = 16
TOPN = 16
TOKENS = 128
NZ, NX = 16, 4
CHIPS = NZ * NX
DEVICES = 2 * CHIPS
PR, QR = 128, 224
VAL, HI, CMP = 0, 128, 192
WIN = 320
P_HALF = ((0, 64), (64, 128))
Q_HALF = ((0, 112), (112, 224))
MESH = pl.DeviceIdType.MESH
SCALE2 = DK**-0.5 * 1.4426950408889634
BF, F32 = jnp.bfloat16, jnp.float32
VMEM_LIMIT = 56 * 2**20


def pooled(rows, gains, mixing):
    summed = jnp.sum(rows.astype(F32).reshape(4, CMP_BLOCK, rows.shape[1]) * gains.astype(F32)[None], axis=1)
    return summed


def compressed(rows_of, gains, mixing):
    both = jnp.concatenate([pooled(rows_of[r], gains, mixing) for r in (0, 1)], axis=0)
    return jnp.dot(both.astype(BF), mixing, preferred_element_type=F32)


def paired_high(k):
    return jnp.concatenate([k[0:64, 128:192], k[64:128, 128:192]], axis=1)


def fused_kernel(sel, q_in, keys_in, values_in, gates_in, pos_k_in, pos_v_in, mix_k_in, mix_v_in, out,
                 q, keys, values, gates, pos_k, pos_v, mix_k, mix_v,
                 gp, gq, win, span, qs, gate_rows, acc, kx, vx, bias,
                 pz, qz, px, qx, d2d, send, lsem, wrecv, wsend):
    me = lax.axis_index("ctx")
    z, x, c = me // 8, (me // 2) % 4, me % 2
    chip = me // 2

    def dev(zz, xx):
        return ((zz + NZ) % NZ) * 8 + ((xx + NX) % NX) * 2 + c

    def slot(zz, xx):
        return c * CHIPS + ((zz + 2 * NZ) % NZ) * NX + (xx + NX) % NX

    def zrow(zz):
        return pl.ds(c * CHIPS + ((zz + 2 * NZ) % NZ) * NX, NX)

    zn = [dev(z + 1, x), dev(z - 1, x)]
    xn = [dev(z, x + 1), dev(z, x - 1)]
    other = me + 1 - 2 * c

    def chip_dev(offset):
        return (chip + offset + CHIPS) % CHIPS * 2 + c

    across = dev(z, x + 2)
    near = [chip_dev(o) for o in (1, 2, -1, -2)]
    ins = (keys_in, values_in, pos_k_in, pos_v_in, mix_k_in, mix_v_in, gates_in, q_in)
    staged = (keys, values, pos_k, pos_v, mix_k, mix_v, gates, q)
    local = [pltpu.make_async_copy(r, v, lsem.at[i]) for i, (r, v) in enumerate(zip(ins, staged))]
    for cp in local:
        cp.start()
    bar = pltpu.get_barrier_semaphore()
    for d in (*zn, *xn, across, other, *near):
        pl.semaphore_signal(bar, inc=1, device_id={"ctx": d}, device_id_type=MESH)
    me_s = slot(z, x)
    local[0].wait()
    row = keys[0].astype(F32).T.astype(BF)
    gp[me_s] = row[:, 0:128]
    pl.semaphore_wait(bar, 10)

    def remote(ref, d, ss, rs, dst=None):
        return pltpu.make_async_remote_copy(
            src_ref=ref, dst_ref=ref if dst is None else dst, send_sem=ss, recv_sem=rs,
            device_id={"ctx": d}, device_id_type=MESH,
        )

    def part(buf, s, rows):
        return buf.at[s] if rows is None else buf.at[s, rows[0] : rows[1]]

    def sp(s, rows, d, rs):
        remote(part(gp, s, rows), d, send.at[0], rs).start()

    def sq(s, rows, d, rs):
        remote(part(gq, s, rows), d, send.at[1], rs).start()

    def wp(s, rows, rs):
        remote(part(gp, s, rows), other, send.at[0], rs).wait_recv()

    def wq(s, rows, rs):
        remote(part(gq, s, rows), other, send.at[1], rs).wait_recv()

    def zsend_p(zz, r, d, k, half):
        sp(slot(zz, x + r), P_HALF[d] if half else None, zn[d], pz.at[d, k, r])

    def zsend_q(zz, d, k, half):
        sq(slot(zz, x), Q_HALF[d] if half else None, zn[d], qz.at[d, k])

    def xsend_q(zz, t, late=False):
        if late:
            sq(slot(zz, x), None, across, qx.at[t, 2])
        for d in (0, 1):
            sq(slot(zz, x), None, xn[d], qx.at[t, d])

    def d2d_p(zz):
        remote(gp.at[zrow(zz)], other, send.at[2], d2d.at[0]).start()

    def d2d_q(zz):
        remote(gq.at[zrow(zz)], other, send.at[3], d2d.at[1]).start()

    sp(me_s, None, across, px.at[2])
    for d in (0, 1):
        sp(me_s, None, xn[d], px.at[d])
    for d in (0, 1):
        zsend_p(z, 0, d, 1, False)
    for cp in local[1:6]:
        cp.wait()
    last_row = keys[1].astype(F32).T.astype(BF)
    rows = (row, last_row)
    gq[me_s, VAL : VAL + 128] = values[0]
    gq[me_s, HI : HI + 64] = paired_high(row)
    ck = compressed(rows, pos_k[...], mix_k[...])
    cv = compressed(values, pos_v[...], mix_v[...])
    gq[me_s, CMP : CMP + 16] = jnp.concatenate([ck[:, 0:128], cv], axis=0).astype(BF)
    hi = jnp.concatenate([ck[:, 128:192], jnp.zeros((8, 64), F32)], axis=1)
    gq[me_s, CMP + 16 : CMP + 32] = jnp.concatenate([hi, jnp.zeros((8, 128), F32)], axis=0).astype(BF)
    for d in (0, 1):
        zsend_q(z, d, 1, False)
    xsend_q(z, 0)
    for r in (0, 1):
        span[r, 0:128] = rows[r][:, 0:128]
        span[r, 128:256] = values[r]
        span[r, 256:320] = paired_high(rows[r])
    win[c] = span[1]
    for o in (1, 2):
        wrapped = jnp.where(chip + o >= CHIPS, 0, 1)
        remote(span.at[wrapped], near[o - 1], wsend.at[o], wrecv.at[o], win.at[2 * o + c]).start()
    remote(win.at[c], other, wsend.at[0], wrecv.at[0]).start()
    for d, r in ((0, 3), (1, 1)):
        wp(slot(z, x + r), None, px.at[d])
        for e in (0, 1):
            zsend_p(z, r, e, 1, False)
    wp(slot(z, x + 2), None, px.at[2])
    for e in (0, 1):
        zsend_p(z, 2, e, 1, False)
    d2d_p(z)
    for cp in local[6:]:
        cp.wait()
    prepare(q, gates, qs, gate_rows, vx)

    def qx_full(zz, t, late=False):
        for d, r in ((0, 3), (1, 1)):
            wq(slot(zz, x + r), None, qx.at[t, d])
            if late:
                continue
            sq(slot(zz, x + r), Q_HALF[d], xn[d], qx.at[t, 2 + d])

    def qx_half(zz, t, late=False):
        if late:
            wq(slot(zz, x + 2), None, qx.at[t, 2])
        for d in () if late else (0, 1):
            wq(slot(zz, x + 2), Q_HALF[d], qx.at[t, 2 + d])
        d2d_q(zz)

    def at_z(d, k):
        return z - k if d == 0 else z + k

    def at_t(d, k):
        return k if d == 0 else 8 + k

    def step(k, last):
        for d in (0, 1):
            wq(slot(at_z(d, k), x), None, qz.at[d, k])
            zsend_q(at_z(d, k), d, k + 1, last)
            xsend_q(at_z(d, k), at_t(d, k))
        for r in (0, 3, 1, 2):
            for d in (0, 1):
                wp(slot(at_z(d, k), x + r), None, pz.at[d, k, r])
                zsend_p(at_z(d, k), r, d, k + 1, last)
        for d in (0, 1):
            d2d_p(at_z(d, k))

    def lag1(k):
        for d in (0, 1):
            qx_full(at_z(d, k), at_t(d, k))

    def lag2(k):
        for d in (0, 1):
            qx_half(at_z(d, k), at_t(d, k))

    step(1, False)
    qx_full(z, 0)
    step(2, False)
    lag1(1)
    qx_half(z, 0)
    for o in (1, 2):
        remote(win.at[2 * o + c], other, wsend.at[o], wrecv.at[o]).wait_recv()
        remote(win.at[2 * o + c], other, wsend.at[2 + o], wrecv.at[2 + o]).start()

    for o in (0, 1, 2):
        ref = win.at[2 * o + 1 - c]
        remote(ref, other, wsend.at[0], wrecv.at[o if o == 0 else 2 + o]).wait_recv()
    window_keys(win, kx.at[0], vx.at[0], bias, c)

    def loop(k, carry):
        step(k, False)
        for i in (0, 1):
            window_heads(2 * (k - 3) + i, qs, gate_rows, acc, kx.at[0], vx.at[0], bias)
        lag1(k - 1)
        lag2(k - 2)
        return carry

    lax.fori_loop(3, 7, loop, 0)
    step(7, True)
    lag1(6)
    lag2(5)
    for d in (0, 1):
        wq(slot(z - 8, x), Q_HALF[d], qz.at[d, 8])
    xsend_q(z - 8, 8, True)
    for r in (0, 3, 1, 2):
        for d in (0, 1):
            wp(slot(z - 8, x + r), P_HALF[d], pz.at[d, 8, r])
    d2d_p(z - 8)
    lag1(7)
    lag2(6)
    qx_full(z - 8, 8, True)
    lag2(7)
    qx_half(z - 8, 8, True)
    theirs = pl.ds((1 - c) * CHIPS, CHIPS)
    for n, buf in enumerate((gp, gq)):
        remote(buf.at[theirs], other, send.at[2 + n], d2d.at[n]).wait_recv()
    compressed_part(gq, qs, gate_rows, acc, kx.at[1], vx.at[1], bias, me)
    selected_part(sel, gp, gq, win, qs, gate_rows, acc, kx, vx, out, c)
    for n, buf in enumerate((gp, gq)):
        remote(buf.at[0 : CHIPS - 1], other, send.at[n], d2d.at[n]).wait_send()
        remote(buf.at[0:CHIPS], other, send.at[2 + n], d2d.at[n]).wait_send()
    for i in range(5):
        remote(win.at[0], other, wsend.at[i], wrecv.at[0]).wait_send()


def mixed(query_rows, key_rows, value_rows, bias):
    heads, tokens = query_rows.shape[0], query_rows.shape[1]
    count = key_rows.shape[0]
    scores = lax.dot_general(
        query_rows.reshape(heads * tokens, 256), key_rows, (((1,), (1,)), ((), ())), preferred_element_type=F32
    )
    scores = scores.reshape(heads, tokens, count) + bias[None]
    highest = jnp.max(scores, axis=2, keepdims=True)
    weights = jnp.exp2((scores - highest) * SCALE2).astype(BF)
    both = jnp.dot(weights.reshape(heads * tokens, count), value_rows, preferred_element_type=F32)
    return (both[:, 0:128] / both[:, 128:256]).reshape(heads, tokens, DV)


def prepare(q, gates, qs, gate_rows, vx):
    none = jnp.zeros((TOKENS, 64), BF)
    for h in range(HEADS):
        qs[h] = jnp.concatenate([q[:, h * DK : (h + 1) * DK], none], axis=1)
    g = jax.nn.sigmoid(gates[...].astype(F32)).T
    for i in range(3 * HEADS):
        gate_rows[i] = jnp.broadcast_to(g[:, i : i + 1], (TOKENS, DV))
    vx[:, :, 128:256] = jnp.ones((2, vx.shape[1], 128), BF)


def window_keys(win, kx, vx, bias, c):
    for i in range(5):
        back = 4 - i - c
        off = (back + 1) // 2
        core = (2 * off - back) % 2
        piece = 2 * off + core
        rows = slice(128 * i, 128 * (i + 1))
        kx[rows, 0:128] = win[piece, 0:128]
        vx[rows, 0:128] = win[piece, 128:256]
        high = win[piece, 256:320]
        kx[128 * i : 128 * i + 64, 128:256] = high
        kx[128 * i + 64 : 128 * i + 128, 128:256] = pltpu.roll(high, 64, 1)
    count = 5 * TOKENS
    column = lax.broadcasted_iota(jnp.int32, (TOKENS, count), 1)
    token = lax.broadcasted_iota(jnp.int32, (TOKENS, count), 0)
    inside = (column > token) & (column <= 4 * TOKENS + token)
    bias[:, 0:count] = jnp.where(inside, 0.0, -jnp.inf)


def window_heads(i, qs, gate_rows, acc, kx, vx, bias):
    count = 5 * TOKENS
    at = pl.ds(2 * i, 2)
    o = mixed(qs[at], kx[0:count], vx[0:count], bias[:, 0:count])
    acc[at] = o * gate_rows[pl.ds(2 * HEADS + 2 * i, 2)]


def compressed_part(gq, qs, gate_rows, acc, kx, vx, bias, me):
    tile = gq[:, CMP : CMP + 16].astype(F32)
    count = DEVICES * 8
    kx[:, 0:128] = tile[:, 0:8].reshape(count, 128).astype(BF)
    vx[:, 0:128] = tile[:, 8:16].reshape(count, 128).astype(BF)
    kx[:, 128:256] = gq[:, CMP + 16 : CMP + 32].astype(F32)[:, 0:8].reshape(count, 128).astype(BF)
    column = lax.broadcasted_iota(jnp.int32, (TOKENS, count), 1)
    token = lax.broadcasted_iota(jnp.int32, (TOKENS, count), 0)
    where = column // 8
    holder = where % CHIPS * 2 + where // CHIPS
    within = column % 8
    end = jnp.where(within < 4, 0, (holder - me) * TOKENS + (within - 3) * CMP_BLOCK - 1)
    bias[...] = jnp.where(end <= token, 0.0, -jnp.inf)

    def heads(i, carry):
        at = pl.ds(2 * i, 2)
        o = mixed(qs[at], kx[...], vx[...], bias[...])
        acc[at] += o * gate_rows[at]
        return carry

    lax.fori_loop(0, HEADS // 2, heads, 0, unroll=True)


def selected_part(sel, gp, gq, win, qs, gate_rows, acc, key_slots, value_slots, out, c):
    count = TOPN * SEL_BLOCK

    def group(g, carry):
        mine = g // 4
        kx, vx = key_slots.at[g % 2], value_slots.at[g % 2]
        kx[0:64, 0:128] = win[c, pl.ds(pl.multiple_of(mine * 64, 64), 64)]
        vx[0:64, 0:128] = win[c, pl.ds(pl.multiple_of(128 + mine * 64, 64), 64)]
        high = win[c, 256:320]
        kx[0:64, 128:256] = jnp.where(mine == 1, pltpu.roll(high, 64, 1), high)
        for e in range(1, TOPN):
            block = jnp.maximum(sel[g, e], 0)
            odd = block & 1
            s = ((block >> 1) & 1) * CHIPS + (block >> 2)
            second = jnp.broadcast_to(odd, (64, 128)) == 1
            low, rest = gp[s], gq[s]
            high = rest[HI : HI + 64]
            rows = slice(64 * e, 64 * (e + 1))
            kx[rows, 0:128] = jnp.where(second, low[64:128], low[0:64])
            vx[rows, 0:128] = jnp.where(second, rest[64:128], rest[0:64])
            kx[rows, 128:256] = jnp.where(second, pltpu.roll(high, 64, 1), high)
        column = lax.broadcasted_iota(jnp.int32, (QBLOCK, count), 1)
        token = lax.broadcasted_iota(jnp.int32, (QBLOCK, count), 0)
        bad = (column < SEL_BLOCK) & (column > (g % 4) * QBLOCK + token)
        for e in range(1, TOPN):
            bad = bad | ((column // SEL_BLOCK == e) & (jnp.broadcast_to(sel[g, e], (QBLOCK, count)) < 0))
        bias = jnp.where(bad, -jnp.inf, 0.0)
        rows = pl.ds(pl.multiple_of(g * QBLOCK, QBLOCK), QBLOCK)
        o = mixed(qs[:, rows], kx[...], vx[...], bias)
        o = acc[:, rows] + o * gate_rows[HEADS : 2 * HEADS, rows]
        for h in range(HEADS):
            out[rows, h * DV : (h + 1) * DV] = o[h].astype(BF)
        return carry

    lax.fori_loop(0, QBLOCK // 2, group, 0, unroll=True)


def body(queries, keys, values, gate_logits, sel_ids, pos_k, pos_v, mix_k, mix_v):
    dma = pltpu.SemaphoreType.DMA
    turned = (
        queries, keys.transpose(0, 2, 1), values, gate_logits.transpose(1, 0), pos_k, pos_v, mix_k, mix_v
    )
    anywhere = pl.BlockSpec(memory_space=pl.ANY)
    return pl.pallas_call(
        fused_kernel,
        out_shape=jax.ShapeDtypeStruct((TOKENS, HEADS * DV), BF),
        in_specs=[pl.BlockSpec(memory_space=pltpu.SMEM)] + [anywhere] * 8,
        out_specs=pl.BlockSpec(memory_space=pltpu.VMEM),
        scratch_shapes=[
            *(pltpu.VMEM(a.shape, BF) for a in turned),
            pltpu.VMEM((DEVICES, PR, 128), BF),
            pltpu.VMEM((DEVICES, QR, 128), BF),
            pltpu.VMEM((6, WIN, 128), BF),
            pltpu.VMEM((2, WIN, 128), BF),
            pltpu.VMEM((HEADS, TOKENS, 256), BF),
            pltpu.VMEM((3 * HEADS, TOKENS, DV), F32),
            pltpu.VMEM((HEADS, TOKENS, DV), F32),
            pltpu.VMEM((2, 1024, 256), BF),
            pltpu.VMEM((2, 1024, 256), BF),
            pltpu.VMEM((TOKENS, 1024), F32),
            dma((2, 9, 4)),
            dma((2, 9)),
            dma((4,)),
            dma((NZ, 4)),
            dma((2,)),
            dma((4,)),
            dma((8,)),
            dma((5,)),
            dma((5,)),
        ],
        compiler_params=pltpu.CompilerParams(
            collective_id=0, has_side_effects=True, vmem_limit_bytes=VMEM_LIMIT
        ),
    )(sel_ids, *turned)


def solution(mesh):
    in_specs = (
        P("ctx", "grp"),
        P(None, "ctx", "grp"),
        P(None, "ctx", "grp"),
        P("ctx", "grp"),
        P("ctx", "grp"),
        P(None, "grp"),
        P(None, "grp"),
        P(None, "grp"),
        P(None, "grp"),
    )
    return jax.shard_map(body, mesh=mesh, in_specs=in_specs, out_specs=P("ctx", "grp"), check_vma=False)
```

```python
import functools

import jax
import jax.numpy as jnp
from jax import lax
from jax.experimental import pallas as pl
from jax.experimental.pallas import tpu as pltpu
from jax.sharding import PartitionSpec as P

HEADS = 16
DK = 192
DV = 128
CMP_BLOCK = 32
SEL_BLOCK = 64
QBLOCK = 16
TOPN = 16
TOKENS = 128
NZ, NX = 16, 4
CHIPS = NZ * NX
DEVICES = 2 * CHIPS
PR, QR = 128, 224
VAL, HI, CMP = 0, 128, 192
WIN = 320
P_HALF = ((0, 64), (64, 128))
Q_HALF = ((0, 112), (112, 224))
MESH = pl.DeviceIdType.MESH
SCALE2 = DK**-0.5 * 1.4426950408889634
BF, F32 = jnp.bfloat16, jnp.float32
VMEM_LIMIT = 56 * 2**20


def pooled(rows, gains, mixing):
    summed = jnp.sum(rows.astype(F32).reshape(4, CMP_BLOCK, rows.shape[1]) * gains.astype(F32)[None], axis=1)
    return summed


def compressed(rows_of, gains, mixing):
    both = jnp.concatenate([pooled(rows_of[r], gains, mixing) for r in (0, 1)], axis=0)
    return jnp.dot(both.astype(BF), mixing, preferred_element_type=F32)


def paired_high(k):
    return jnp.concatenate([k[0:64, 128:192], k[64:128, 128:192]], axis=1)


def fused_kernel(sel, q_in, keys_in, values_in, gates_in, pos_k_in, pos_v_in, mix_k_in, mix_v_in, out,
                 q, keys, values, gates, pos_k, pos_v, mix_k, mix_v,
                 gp, gq, win, span, qs, gate_rows, acc, kx, vx, bias,
                 pz, qz, px, qx, d2d, send, lsem, wrecv, wsend):
    me = lax.axis_index("ctx")
    z, x, c = me // 8, (me // 2) % 4, me % 2
    chip = me // 2

    def dev(zz, xx):
        return ((zz + NZ) % NZ) * 8 + ((xx + NX) % NX) * 2 + c

    def slot(zz, xx):
        return c * CHIPS + ((zz + 2 * NZ) % NZ) * NX + (xx + NX) % NX

    def zrow(zz):
        return pl.ds(c * CHIPS + ((zz + 2 * NZ) % NZ) * NX, NX)

    zn = [dev(z + 1, x), dev(z - 1, x)]
    xn = [dev(z, x + 1), dev(z, x - 1)]
    other = me + 1 - 2 * c

    def chip_dev(offset):
        return (chip + offset + CHIPS) % CHIPS * 2 + c

    across = dev(z, x + 2)
    near = [chip_dev(o) for o in (1, 2, -1, -2)]
    ins = (keys_in, values_in, pos_k_in, pos_v_in, mix_k_in, mix_v_in, gates_in, q_in)
    staged = (keys, values, pos_k, pos_v, mix_k, mix_v, gates, q)
    local = [pltpu.make_async_copy(r, v, lsem.at[i]) for i, (r, v) in enumerate(zip(ins, staged))]
    for cp in local:
        cp.start()
    bar = pltpu.get_barrier_semaphore()
    for d in (*zn, *xn, across, other, *near):
        pl.semaphore_signal(bar, inc=1, device_id={"ctx": d}, device_id_type=MESH)
    me_s = slot(z, x)
    local[0].wait()
    row = keys[0].astype(F32).T.astype(BF)
    gp[me_s] = row[:, 0:128]
    pl.semaphore_wait(bar, 10)

    def remote(ref, d, ss, rs, dst=None):
        return pltpu.make_async_remote_copy(
            src_ref=ref, dst_ref=ref if dst is None else dst, send_sem=ss, recv_sem=rs,
            device_id={"ctx": d}, device_id_type=MESH,
        )

    def part(buf, s, rows):
        return buf.at[s] if rows is None else buf.at[s, rows[0] : rows[1]]

    def sp(s, rows, d, rs):
        remote(part(gp, s, rows), d, send.at[0], rs).start()

    def sq(s, rows, d, rs):
        remote(part(gq, s, rows), d, send.at[1], rs).start()

    def wp(s, rows, rs):
        remote(part(gp, s, rows), other, send.at[0], rs).wait_recv()

    def wq(s, rows, rs):
        remote(part(gq, s, rows), other, send.at[1], rs).wait_recv()

    def zsend_p(zz, r, d, k, half):
        sp(slot(zz, x + r), P_HALF[d] if half else None, zn[d], pz.at[d, k, r])

    def zsend_q(zz, d, k, half):
        sq(slot(zz, x), Q_HALF[d] if half else None, zn[d], qz.at[d, k])

    def xsend_q(zz, t, late=False):
        if late:
            sq(slot(zz, x), None, across, qx.at[t, 2])
        for d in (0, 1):
            sq(slot(zz, x), None, xn[d], qx.at[t, d])

    def d2d_p(zz):
        remote(gp.at[zrow(zz)], other, send.at[2], d2d.at[0]).start()

    def d2d_q(zz):
        remote(gq.at[zrow(zz)], other, send.at[3], d2d.at[1]).start()

    sp(me_s, None, across, px.at[2])
    for d in (0, 1):
        sp(me_s, None, xn[d], px.at[d])
    for d in (0, 1):
        zsend_p(z, 0, d, 1, False)
    for cp in local[1:6]:
        cp.wait()
    last_row = keys[1].astype(F32).T.astype(BF)
    rows = (row, last_row)
    gq[me_s, VAL : VAL + 128] = values[0]
    gq[me_s, HI : HI + 64] = paired_high(row)
    ck = compressed(rows, pos_k[...], mix_k[...])
    cv = compressed(values, pos_v[...], mix_v[...])
    gq[me_s, CMP : CMP + 16] = jnp.concatenate([ck[:, 0:128], cv], axis=0).astype(BF)
    hi = jnp.concatenate([ck[:, 128:192], jnp.zeros((8, 64), F32)], axis=1)
    gq[me_s, CMP + 16 : CMP + 32] = jnp.concatenate([hi, jnp.zeros((8, 128), F32)], axis=0).astype(BF)
    for d in (0, 1):
        zsend_q(z, d, 1, False)
    xsend_q(z, 0)
    for r in (0, 1):
        span[r, 0:128] = rows[r][:, 0:128]
        span[r, 128:256] = values[r]
        span[r, 256:320] = paired_high(rows[r])
    win[c] = span[1]
    for o in (1, 2):
        wrapped = jnp.where(chip + o >= CHIPS, 0, 1)
        remote(span.at[wrapped], near[o - 1], wsend.at[o], wrecv.at[o], win.at[2 * o + c]).start()
    remote(win.at[c], other, wsend.at[0], wrecv.at[0]).start()
    for d, r in ((0, 3), (1, 1)):
        wp(slot(z, x + r), None, px.at[d])
        for e in (0, 1):
            zsend_p(z, r, e, 1, False)
    wp(slot(z, x + 2), None, px.at[2])
    for e in (0, 1):
        zsend_p(z, 2, e, 1, False)
    d2d_p(z)
    for cp in local[6:]:
        cp.wait()
    prepare(q, gates, qs, gate_rows, vx)

    def qx_full(zz, t, late=False):
        for d, r in ((0, 3), (1, 1)):
            wq(slot(zz, x + r), None, qx.at[t, d])
            if late:
                continue
            sq(slot(zz, x + r), Q_HALF[d], xn[d], qx.at[t, 2 + d])

    def qx_half(zz, t, late=False):
        if late:
            wq(slot(zz, x + 2), None, qx.at[t, 2])
        for d in () if late else (0, 1):
            wq(slot(zz, x + 2), Q_HALF[d], qx.at[t, 2 + d])
        d2d_q(zz)

    def at_z(d, k):
        return z - k if d == 0 else z + k

    def at_t(d, k):
        return k if d == 0 else 8 + k

    def step(k, last, between=()):
        for d in (0, 1):
            wq(slot(at_z(d, k), x), None, qz.at[d, k])
            zsend_q(at_z(d, k), d, k + 1, last)
            xsend_q(at_z(d, k), at_t(d, k))
        for n, r in enumerate((0, 3, 1, 2)):
            for d in (0, 1):
                wp(slot(at_z(d, k), x + r), None, pz.at[d, k, r])
                zsend_p(at_z(d, k), r, d, k + 1, last)
            if n < len(between):
                between[n]()
        for d in (0, 1):
            d2d_p(at_z(d, k))

    def full(d, k):
        return lambda: qx_full(at_z(d, k), at_t(d, k))

    def half(d, k):
        return lambda: qx_half(at_z(d, k), at_t(d, k))

    def lag1(k):
        for d in (0, 1):
            qx_full(at_z(d, k), at_t(d, k))

    def lag2(k):
        for d in (0, 1):
            qx_half(at_z(d, k), at_t(d, k))

    step(1, False, (lambda: qx_full(z, 0),))
    step(2, False, (full(0, 1), full(1, 1)))
    qx_half(z, 0)
    for o in (1, 2):
        remote(win.at[2 * o + c], other, wsend.at[o], wrecv.at[o]).wait_recv()
        remote(win.at[2 * o + c], other, wsend.at[2 + o], wrecv.at[2 + o]).start()

    for o in (0, 1, 2):
        ref = win.at[2 * o + 1 - c]
        remote(ref, other, wsend.at[0], wrecv.at[o if o == 0 else 2 + o]).wait_recv()
    window_keys(win, kx.at[0], vx.at[0], bias, c)

    def loop(k, carry):
        step(k, False, (full(0, k - 1), full(1, k - 1)))
        for i in (0, 1):
            window_heads(2 * (k - 3) + i, qs, gate_rows, acc, kx.at[0], vx.at[0], bias)
        lag2(k - 2)
        return carry

    lax.fori_loop(3, 7, loop, 0)
    step(7, True, (full(0, 6), full(1, 6)))
    lag2(5)
    for d in (0, 1):
        wq(slot(z - 8, x), Q_HALF[d], qz.at[d, 8])
    xsend_q(z - 8, 8, True)
    late = (full(0, 7), full(1, 7), half(0, 6), half(1, 6))
    for n, r in enumerate((0, 3, 1, 2)):
        for d in (0, 1):
            wp(slot(z - 8, x + r), P_HALF[d], pz.at[d, 8, r])
        late[n]()
    d2d_p(z - 8)
    qx_full(z - 8, 8, True)
    lag2(7)
    qx_half(z - 8, 8, True)
    theirs = pl.ds((1 - c) * CHIPS, CHIPS)
    for n, buf in enumerate((gp, gq)):
        remote(buf.at[theirs], other, send.at[2 + n], d2d.at[n]).wait_recv()
    compressed_part(gq, qs, gate_rows, acc, kx.at[1], vx.at[1], bias, me)
    selected_part(sel, gp, gq, win, qs, gate_rows, acc, kx, vx, out, c)
    for n, buf in enumerate((gp, gq)):
        remote(buf.at[0 : CHIPS - 1], other, send.at[n], d2d.at[n]).wait_send()
        remote(buf.at[0:CHIPS], other, send.at[2 + n], d2d.at[n]).wait_send()
    for i in range(5):
        remote(win.at[0], other, wsend.at[i], wrecv.at[0]).wait_send()


def mixed(query_rows, key_rows, value_rows, bias):
    heads, tokens = query_rows.shape[0], query_rows.shape[1]
    count = key_rows.shape[0]
    scores = lax.dot_general(
        query_rows.reshape(heads * tokens, 256), key_rows, (((1,), (1,)), ((), ())), preferred_element_type=F32
    )
    scores = scores.reshape(heads, tokens, count) + bias[None]
    highest = jnp.max(scores, axis=2, keepdims=True)
    weights = jnp.exp2((scores - highest) * SCALE2).astype(BF)
    both = jnp.dot(weights.reshape(heads * tokens, count), value_rows, preferred_element_type=F32)
    return (both[:, 0:128] / both[:, 128:256]).reshape(heads, tokens, DV)


def prepare(q, gates, qs, gate_rows, vx):
    none = jnp.zeros((TOKENS, 64), BF)
    for h in range(HEADS):
        qs[h] = jnp.concatenate([q[:, h * DK : (h + 1) * DK], none], axis=1)
    g = jax.nn.sigmoid(gates[...].astype(F32)).T
    for i in range(3 * HEADS):
        gate_rows[i] = jnp.broadcast_to(g[:, i : i + 1], (TOKENS, DV))
    vx[:, :, 128:256] = jnp.ones((2, vx.shape[1], 128), BF)


def window_keys(win, kx, vx, bias, c):
    for i in range(5):
        back = 4 - i - c
        off = (back + 1) // 2
        core = (2 * off - back) % 2
        piece = 2 * off + core
        rows = slice(128 * i, 128 * (i + 1))
        kx[rows, 0:128] = win[piece, 0:128]
        vx[rows, 0:128] = win[piece, 128:256]
        high = win[piece, 256:320]
        kx[128 * i : 128 * i + 64, 128:256] = high
        kx[128 * i + 64 : 128 * i + 128, 128:256] = pltpu.roll(high, 64, 1)
    count = 5 * TOKENS
    column = lax.broadcasted_iota(jnp.int32, (TOKENS, count), 1)
    token = lax.broadcasted_iota(jnp.int32, (TOKENS, count), 0)
    inside = (column > token) & (column <= 4 * TOKENS + token)
    bias[:, 0:count] = jnp.where(inside, 0.0, -jnp.inf)


def window_heads(i, qs, gate_rows, acc, kx, vx, bias):
    count = 5 * TOKENS
    at = pl.ds(2 * i, 2)
    o = mixed(qs[at], kx[0:count], vx[0:count], bias[:, 0:count])
    acc[at] = o * gate_rows[pl.ds(2 * HEADS + 2 * i, 2)]


def compressed_part(gq, qs, gate_rows, acc, kx, vx, bias, me):
    tile = gq[:, CMP : CMP + 16].astype(F32)
    count = DEVICES * 8
    kx[:, 0:128] = tile[:, 0:8].reshape(count, 128).astype(BF)
    vx[:, 0:128] = tile[:, 8:16].reshape(count, 128).astype(BF)
    kx[:, 128:256] = gq[:, CMP + 16 : CMP + 32].astype(F32)[:, 0:8].reshape(count, 128).astype(BF)
    column = lax.broadcasted_iota(jnp.int32, (TOKENS, count), 1)
    token = lax.broadcasted_iota(jnp.int32, (TOKENS, count), 0)
    where = column // 8
    holder = where % CHIPS * 2 + where // CHIPS
    within = column % 8
    end = jnp.where(within < 4, 0, (holder - me) * TOKENS + (within - 3) * CMP_BLOCK - 1)
    bias[...] = jnp.where(end <= token, 0.0, -jnp.inf)

    def heads(i, carry):
        at = pl.ds(2 * i, 2)
        o = mixed(qs[at], kx[...], vx[...], bias[...])
        acc[at] += o * gate_rows[at]
        return carry

    lax.fori_loop(0, HEADS // 2, heads, 0, unroll=True)


def selected_part(sel, gp, gq, win, qs, gate_rows, acc, key_slots, value_slots, out, c):
    count = TOPN * SEL_BLOCK

    def group(g, carry):
        mine = g // 4
        kx, vx = key_slots.at[g % 2], value_slots.at[g % 2]
        kx[0:64, 0:128] = win[c, pl.ds(pl.multiple_of(mine * 64, 64), 64)]
        vx[0:64, 0:128] = win[c, pl.ds(pl.multiple_of(128 + mine * 64, 64), 64)]
        high = win[c, 256:320]
        kx[0:64, 128:256] = jnp.where(mine == 1, pltpu.roll(high, 64, 1), high)
        for e in range(1, TOPN):
            block = jnp.maximum(sel[g, e], 0)
            odd = block & 1
            s = ((block >> 1) & 1) * CHIPS + (block >> 2)
            second = jnp.broadcast_to(odd, (64, 128)) == 1
            low, rest = gp[s], gq[s]
            high = rest[HI : HI + 64]
            rows = slice(64 * e, 64 * (e + 1))
            kx[rows, 0:128] = jnp.where(second, low[64:128], low[0:64])
            vx[rows, 0:128] = jnp.where(second, rest[64:128], rest[0:64])
            kx[rows, 128:256] = jnp.where(second, pltpu.roll(high, 64, 1), high)
        column = lax.broadcasted_iota(jnp.int32, (QBLOCK, count), 1)
        token = lax.broadcasted_iota(jnp.int32, (QBLOCK, count), 0)
        bad = (column < SEL_BLOCK) & (column > (g % 4) * QBLOCK + token)
        for e in range(1, TOPN):
            bad = bad | ((column // SEL_BLOCK == e) & (jnp.broadcast_to(sel[g, e], (QBLOCK, count)) < 0))
        bias = jnp.where(bad, -jnp.inf, 0.0)
        rows = pl.ds(pl.multiple_of(g * QBLOCK, QBLOCK), QBLOCK)
        o = mixed(qs[:, rows], kx[...], vx[...], bias)
        o = acc[:, rows] + o * gate_rows[HEADS : 2 * HEADS, rows]
        for h in range(HEADS):
            out[rows, h * DV : (h + 1) * DV] = o[h].astype(BF)
        return carry

    lax.fori_loop(0, QBLOCK // 2, group, 0, unroll=True)


def body(queries, keys, values, gate_logits, sel_ids, pos_k, pos_v, mix_k, mix_v):
    dma = pltpu.SemaphoreType.DMA
    turned = (
        queries, keys.transpose(0, 2, 1), values, gate_logits.transpose(1, 0), pos_k, pos_v, mix_k, mix_v
    )
    anywhere = pl.BlockSpec(memory_space=pl.ANY)
    return pl.pallas_call(
        fused_kernel,
        out_shape=jax.ShapeDtypeStruct((TOKENS, HEADS * DV), BF),
        in_specs=[pl.BlockSpec(memory_space=pltpu.SMEM)] + [anywhere] * 8,
        out_specs=pl.BlockSpec(memory_space=pltpu.VMEM),
        scratch_shapes=[
            *(pltpu.VMEM(a.shape, BF) for a in turned),
            pltpu.VMEM((DEVICES, PR, 128), BF),
            pltpu.VMEM((DEVICES, QR, 128), BF),
            pltpu.VMEM((6, WIN, 128), BF),
            pltpu.VMEM((2, WIN, 128), BF),
            pltpu.VMEM((HEADS, TOKENS, 256), BF),
            pltpu.VMEM((3 * HEADS, TOKENS, DV), F32),
            pltpu.VMEM((HEADS, TOKENS, DV), F32),
            pltpu.VMEM((2, 1024, 256), BF),
            pltpu.VMEM((2, 1024, 256), BF),
            pltpu.VMEM((TOKENS, 1024), F32),
            dma((2, 9, 4)),
            dma((2, 9)),
            dma((4,)),
            dma((NZ, 4)),
            dma((2,)),
            dma((4,)),
            dma((8,)),
            dma((5,)),
            dma((5,)),
        ],
        compiler_params=pltpu.CompilerParams(
            collective_id=0, has_side_effects=True, vmem_limit_bytes=VMEM_LIMIT
        ),
    )(sel_ids, *turned)


def solution(mesh):
    in_specs = (
        P("ctx", "grp"),
        P(None, "ctx", "grp"),
        P(None, "ctx", "grp"),
        P("ctx", "grp"),
        P("ctx", "grp"),
        P(None, "grp"),
        P(None, "grp"),
        P(None, "grp"),
        P(None, "grp"),
    )
    return jax.shard_map(body, mesh=mesh, in_specs=in_specs, out_specs=P("ctx", "grp"), check_vma=False)
```

```python
import functools

import jax
import jax.numpy as jnp
from jax import lax
from jax.experimental import pallas as pl
from jax.experimental.pallas import tpu as pltpu
from jax.sharding import PartitionSpec as P

HEADS = 16
DK = 192
DV = 128
CMP_BLOCK = 32
SEL_BLOCK = 64
QBLOCK = 16
TOPN = 16
TOKENS = 128
NZ, NX = 16, 4
CHIPS = NZ * NX
DEVICES = 2 * CHIPS
PR, QR = 128, 224
VAL, HI, CMP = 0, 128, 192
WIN = 320
P_HALF = ((0, 64), (64, 128))
Q_HALF = ((0, 112), (112, 224))
MESH = pl.DeviceIdType.MESH
SCALE2 = DK**-0.5 * 1.4426950408889634
BF, F32 = jnp.bfloat16, jnp.float32
VMEM_LIMIT = 56 * 2**20


def pooled(rows, gains, mixing):
    summed = jnp.sum(rows.astype(F32).reshape(4, CMP_BLOCK, rows.shape[1]) * gains.astype(F32)[None], axis=1)
    return summed


def compressed(rows_of, gains, mixing):
    both = jnp.concatenate([pooled(rows_of[r], gains, mixing) for r in (0, 1)], axis=0)
    return jnp.dot(both.astype(BF), mixing, preferred_element_type=F32)


def paired_high(k):
    return jnp.concatenate([k[0:64, 128:192], k[64:128, 128:192]], axis=1)


def fused_kernel(sel, q_in, keys_in, values_in, gates_in, pos_k_in, pos_v_in, mix_k_in, mix_v_in, out,
                 q, keys, values, gates, pos_k, pos_v, mix_k, mix_v,
                 gp, gq, win, span, qs, gate_rows, acc, kx, vx, bias,
                 pz, qz, px, qx, d2d, send, lsem, wrecv, wsend):
    me = lax.axis_index("ctx")
    z, x, c = me // 8, (me // 2) % 4, me % 2
    chip = me // 2

    def dev(zz, xx):
        return ((zz + NZ) % NZ) * 8 + ((xx + NX) % NX) * 2 + c

    def slot(zz, xx):
        return c * CHIPS + ((zz + 2 * NZ) % NZ) * NX + (xx + NX) % NX

    def zrow(zz):
        return pl.ds(c * CHIPS + ((zz + 2 * NZ) % NZ) * NX, NX)

    zn = [dev(z + 1, x), dev(z - 1, x)]
    xn = [dev(z, x + 1), dev(z, x - 1)]
    other = me + 1 - 2 * c

    def chip_dev(offset):
        return (chip + offset + CHIPS) % CHIPS * 2 + c

    across = dev(z, x + 2)
    near = [chip_dev(o) for o in (1, 2, -1, -2)]
    ins = (keys_in, values_in, pos_k_in, pos_v_in, mix_k_in, mix_v_in, gates_in, q_in)
    staged = (keys, values, pos_k, pos_v, mix_k, mix_v, gates, q)
    local = [pltpu.make_async_copy(r, v, lsem.at[i]) for i, (r, v) in enumerate(zip(ins, staged))]
    for cp in local:
        cp.start()
    bar = pltpu.get_barrier_semaphore()
    for d in (*zn, *xn, across, other, *near):
        pl.semaphore_signal(bar, inc=1, device_id={"ctx": d}, device_id_type=MESH)
    me_s = slot(z, x)
    local[0].wait()
    row = keys[0].astype(F32).T.astype(BF)
    gp[me_s] = row[:, 0:128]
    pl.semaphore_wait(bar, 10)

    def remote(ref, d, ss, rs, dst=None):
        return pltpu.make_async_remote_copy(
            src_ref=ref, dst_ref=ref if dst is None else dst, send_sem=ss, recv_sem=rs,
            device_id={"ctx": d}, device_id_type=MESH,
        )

    def part(buf, s, rows):
        return buf.at[s] if rows is None else buf.at[s, rows[0] : rows[1]]

    def sp(s, rows, d, rs):
        remote(part(gp, s, rows), d, send.at[0], rs).start()

    def sq(s, rows, d, rs):
        remote(part(gq, s, rows), d, send.at[1], rs).start()

    def wp(s, rows, rs):
        remote(part(gp, s, rows), other, send.at[0], rs).wait_recv()

    def wq(s, rows, rs):
        remote(part(gq, s, rows), other, send.at[1], rs).wait_recv()

    def zsend_p(zz, r, d, k, half):
        sp(slot(zz, x + r), P_HALF[d] if half else None, zn[d], pz.at[d, k, r])

    def zsend_q(zz, d, k, half):
        sq(slot(zz, x), Q_HALF[d] if half else None, zn[d], qz.at[d, k])

    def xsend_q(zz, t, late=False):
        if late:
            sq(slot(zz, x), None, across, qx.at[t, 2])
        for d in (0, 1):
            sq(slot(zz, x), None, xn[d], qx.at[t, d])

    def d2d_p(zz):
        remote(gp.at[zrow(zz)], other, send.at[2], d2d.at[0]).start()

    def d2d_q(zz):
        remote(gq.at[zrow(zz)], other, send.at[3], d2d.at[1]).start()

    sp(me_s, None, across, px.at[2])
    for d in (0, 1):
        sp(me_s, None, xn[d], px.at[d])
    for d in (0, 1):
        zsend_p(z, 0, d, 1, False)
    for cp in local[1:6]:
        cp.wait()
    last_row = keys[1].astype(F32).T.astype(BF)
    rows = (row, last_row)
    gq[me_s, VAL : VAL + 128] = values[0]
    gq[me_s, HI : HI + 64] = paired_high(row)
    ck = compressed(rows, pos_k[...], mix_k[...])
    cv = compressed(values, pos_v[...], mix_v[...])
    gq[me_s, CMP : CMP + 16] = jnp.concatenate([ck[:, 0:128], cv], axis=0).astype(BF)
    hi = jnp.concatenate([ck[:, 128:192], jnp.zeros((8, 64), F32)], axis=1)
    gq[me_s, CMP + 16 : CMP + 32] = jnp.concatenate([hi, jnp.zeros((8, 128), F32)], axis=0).astype(BF)
    for d in (0, 1):
        zsend_q(z, d, 1, False)
    xsend_q(z, 0)
    for r in (0, 1):
        span[r, 0:128] = rows[r][:, 0:128]
        span[r, 128:256] = values[r]
        span[r, 256:320] = paired_high(rows[r])
    win[c] = span[1]
    for o in (1, 2):
        wrapped = jnp.where(chip + o >= CHIPS, 0, 1)
        remote(span.at[wrapped], near[o - 1], wsend.at[o], wrecv.at[o], win.at[2 * o + c]).start()
    remote(win.at[c], other, wsend.at[0], wrecv.at[0]).start()
    for d, r in ((0, 3), (1, 1)):
        wp(slot(z, x + r), None, px.at[d])
        for e in (0, 1):
            zsend_p(z, r, e, 1, False)
    wp(slot(z, x + 2), None, px.at[2])
    for e in (0, 1):
        zsend_p(z, 2, e, 1, False)
    d2d_p(z)
    for cp in local[6:]:
        cp.wait()
    prepare(q, gates, qs, gate_rows, vx)

    def qx_full(zz, t, late=False):
        for d, r in ((0, 3), (1, 1)):
            wq(slot(zz, x + r), None, qx.at[t, d])
            if late:
                continue
            sq(slot(zz, x + r), Q_HALF[d], xn[d], qx.at[t, 2 + d])

    def qx_half(zz, t, late=False):
        if late:
            wq(slot(zz, x + 2), None, qx.at[t, 2])
        for d in () if late else (0, 1):
            wq(slot(zz, x + 2), Q_HALF[d], qx.at[t, 2 + d])
        d2d_q(zz)

    def at_z(d, k):
        return z - k if d == 0 else z + k

    def at_t(d, k):
        return k if d == 0 else 8 + k

    def step(k, last, between=()):
        for d in (0, 1):
            wq(slot(at_z(d, k), x), None, qz.at[d, k])
            zsend_q(at_z(d, k), d, k + 1, last)
            xsend_q(at_z(d, k), at_t(d, k))
        for n, r in enumerate((0, 3, 1, 2)):
            for d in (0, 1):
                wp(slot(at_z(d, k), x + r), None, pz.at[d, k, r])
                zsend_p(at_z(d, k), r, d, k + 1, last)
            if n < len(between):
                between[n]()
        for d in (0, 1):
            d2d_p(at_z(d, k))

    def full(d, k):
        return lambda: qx_full(at_z(d, k), at_t(d, k))

    def half(d, k):
        return lambda: qx_half(at_z(d, k), at_t(d, k))

    def lag1(k):
        for d in (0, 1):
            qx_full(at_z(d, k), at_t(d, k))

    def lag2(k):
        for d in (0, 1):
            qx_half(at_z(d, k), at_t(d, k))

    step(1, False, (lambda: qx_full(z, 0),))
    step(2, False, (full(0, 1), full(1, 1)))
    qx_half(z, 0)
    for o in (1, 2):
        remote(win.at[2 * o + c], other, wsend.at[o], wrecv.at[o]).wait_recv()
        remote(win.at[2 * o + c], other, wsend.at[2 + o], wrecv.at[2 + o]).start()

    for o in (0, 1, 2):
        ref = win.at[2 * o + 1 - c]
        remote(ref, other, wsend.at[0], wrecv.at[o if o == 0 else 2 + o]).wait_recv()
    window_keys(win, kx.at[0], vx.at[0], bias, c)

    def loop(k, carry):
        step(k, False, (full(0, k - 1), full(1, k - 1)))
        for i in (0, 1):
            window_heads(2 * (k - 3) + i, qs, gate_rows, acc, kx.at[0], vx.at[0], bias)
        lag2(k - 2)
        return carry

    lax.fori_loop(3, 7, loop, 0)
    step(7, True, (full(0, 6), full(1, 6)))
    lag2(5)
    for d in (0, 1):
        wq(slot(z - 8, x), Q_HALF[d], qz.at[d, 8])
    xsend_q(z - 8, 8, True)
    late = (full(0, 7), full(1, 7), half(0, 6), half(1, 6))
    for n, r in enumerate((0, 3, 1, 2)):
        for d in (0, 1):
            wp(slot(z - 8, x + r), P_HALF[d], pz.at[d, 8, r])
        late[n]()
    d2d_p(z - 8)
    qx_full(z - 8, 8, True)
    lag2(7)
    qx_half(z - 8, 8, True)
    theirs = pl.ds((1 - c) * CHIPS, CHIPS)
    remote(gq.at[theirs], other, send.at[3], d2d.at[1]).wait_recv()
    compressed_part(gq, qs, gate_rows, acc, kx.at[1], vx.at[1], bias, me)
    remote(gp.at[theirs], other, send.at[2], d2d.at[0]).wait_recv()
    selected_part(sel, gp, gq, win, qs, gate_rows, acc, kx, vx, out, c)
    for n, buf in enumerate((gp, gq)):
        remote(buf.at[0 : CHIPS - 1], other, send.at[n], d2d.at[n]).wait_send()
        remote(buf.at[0:CHIPS], other, send.at[2 + n], d2d.at[n]).wait_send()
    for i in range(5):
        remote(win.at[0], other, wsend.at[i], wrecv.at[0]).wait_send()


def mixed(query_rows, key_rows, value_rows, bias):
    heads, tokens = query_rows.shape[0], query_rows.shape[1]
    count = key_rows.shape[0]
    scores = lax.dot_general(
        query_rows.reshape(heads * tokens, 256), key_rows, (((1,), (1,)), ((), ())), preferred_element_type=F32
    )
    scores = scores.reshape(heads, tokens, count) + bias[None]
    highest = jnp.max(scores, axis=2, keepdims=True)
    weights = jnp.exp2((scores - highest) * SCALE2).astype(BF)
    both = jnp.dot(weights.reshape(heads * tokens, count), value_rows, preferred_element_type=F32)
    return (both[:, 0:128] / both[:, 128:256]).reshape(heads, tokens, DV)


def prepare(q, gates, qs, gate_rows, vx):
    none = jnp.zeros((TOKENS, 64), BF)
    for h in range(HEADS):
        qs[h] = jnp.concatenate([q[:, h * DK : (h + 1) * DK], none], axis=1)
    g = jax.nn.sigmoid(gates[...].astype(F32)).T
    for i in range(3 * HEADS):
        gate_rows[i] = jnp.broadcast_to(g[:, i : i + 1], (TOKENS, DV))
    vx[:, :, 128:256] = jnp.ones((2, vx.shape[1], 128), BF)


def window_keys(win, kx, vx, bias, c):
    for i in range(5):
        back = 4 - i - c
        off = (back + 1) // 2
        core = (2 * off - back) % 2
        piece = 2 * off + core
        rows = slice(128 * i, 128 * (i + 1))
        kx[rows, 0:128] = win[piece, 0:128]
        vx[rows, 0:128] = win[piece, 128:256]
        high = win[piece, 256:320]
        kx[128 * i : 128 * i + 64, 128:256] = high
        kx[128 * i + 64 : 128 * i + 128, 128:256] = pltpu.roll(high, 64, 1)
    count = 5 * TOKENS
    column = lax.broadcasted_iota(jnp.int32, (TOKENS, count), 1)
    token = lax.broadcasted_iota(jnp.int32, (TOKENS, count), 0)
    inside = (column > token) & (column <= 4 * TOKENS + token)
    bias[:, 0:count] = jnp.where(inside, 0.0, -jnp.inf)


def window_heads(i, qs, gate_rows, acc, kx, vx, bias):
    count = 5 * TOKENS
    at = pl.ds(2 * i, 2)
    o = mixed(qs[at], kx[0:count], vx[0:count], bias[:, 0:count])
    acc[at] = o * gate_rows[pl.ds(2 * HEADS + 2 * i, 2)]


def compressed_part(gq, qs, gate_rows, acc, kx, vx, bias, me):
    tile = gq[:, CMP : CMP + 16].astype(F32)
    count = DEVICES * 8
    kx[:, 0:128] = tile[:, 0:8].reshape(count, 128).astype(BF)
    vx[:, 0:128] = tile[:, 8:16].reshape(count, 128).astype(BF)
    kx[:, 128:256] = gq[:, CMP + 16 : CMP + 32].astype(F32)[:, 0:8].reshape(count, 128).astype(BF)
    column = lax.broadcasted_iota(jnp.int32, (TOKENS, count), 1)
    token = lax.broadcasted_iota(jnp.int32, (TOKENS, count), 0)
    where = column // 8
    holder = where % CHIPS * 2 + where // CHIPS
    within = column % 8
    end = jnp.where(within < 4, 0, (holder - me) * TOKENS + (within - 3) * CMP_BLOCK - 1)
    bias[...] = jnp.where(end <= token, 0.0, -jnp.inf)

    def heads(i, carry):
        at = pl.ds(2 * i, 2)
        o = mixed(qs[at], kx[...], vx[...], bias[...])
        acc[at] += o * gate_rows[at]
        return carry

    lax.fori_loop(0, HEADS // 2, heads, 0, unroll=True)


def selected_part(sel, gp, gq, win, qs, gate_rows, acc, key_slots, value_slots, out, c):
    count = TOPN * SEL_BLOCK

    def group(g, carry):
        mine = g // 4
        kx, vx = key_slots.at[g % 2], value_slots.at[g % 2]
        kx[0:64, 0:128] = win[c, pl.ds(pl.multiple_of(mine * 64, 64), 64)]
        vx[0:64, 0:128] = win[c, pl.ds(pl.multiple_of(128 + mine * 64, 64), 64)]
        high = win[c, 256:320]
        kx[0:64, 128:256] = jnp.where(mine == 1, pltpu.roll(high, 64, 1), high)
        for e in range(1, TOPN):
            block = jnp.maximum(sel[g, e], 0)
            odd = block & 1
            s = ((block >> 1) & 1) * CHIPS + (block >> 2)
            second = jnp.broadcast_to(odd, (64, 128)) == 1
            low, rest = gp[s], gq[s]
            high = rest[HI : HI + 64]
            rows = slice(64 * e, 64 * (e + 1))
            kx[rows, 0:128] = jnp.where(second, low[64:128], low[0:64])
            vx[rows, 0:128] = jnp.where(second, rest[64:128], rest[0:64])
            kx[rows, 128:256] = jnp.where(second, pltpu.roll(high, 64, 1), high)
        column = lax.broadcasted_iota(jnp.int32, (QBLOCK, count), 1)
        token = lax.broadcasted_iota(jnp.int32, (QBLOCK, count), 0)
        bad = (column < SEL_BLOCK) & (column > (g % 4) * QBLOCK + token)
        for e in range(1, TOPN):
            bad = bad | ((column // SEL_BLOCK == e) & (jnp.broadcast_to(sel[g, e], (QBLOCK, count)) < 0))
        bias = jnp.where(bad, -jnp.inf, 0.0)
        rows = pl.ds(pl.multiple_of(g * QBLOCK, QBLOCK), QBLOCK)
        o = mixed(qs[:, rows], kx[...], vx[...], bias)
        o = acc[:, rows] + o * gate_rows[HEADS : 2 * HEADS, rows]
        for h in range(HEADS):
            out[rows, h * DV : (h + 1) * DV] = o[h].astype(BF)
        return carry

    lax.fori_loop(0, QBLOCK // 2, group, 0, unroll=True)


def body(queries, keys, values, gate_logits, sel_ids, pos_k, pos_v, mix_k, mix_v):
    dma = pltpu.SemaphoreType.DMA
    turned = (
        queries, keys.transpose(0, 2, 1), values, gate_logits.transpose(1, 0), pos_k, pos_v, mix_k, mix_v
    )
    anywhere = pl.BlockSpec(memory_space=pl.ANY)
    return pl.pallas_call(
        fused_kernel,
        out_shape=jax.ShapeDtypeStruct((TOKENS, HEADS * DV), BF),
        in_specs=[pl.BlockSpec(memory_space=pltpu.SMEM)] + [anywhere] * 8,
        out_specs=pl.BlockSpec(memory_space=pltpu.VMEM),
        scratch_shapes=[
            *(pltpu.VMEM(a.shape, BF) for a in turned),
            pltpu.VMEM((DEVICES, PR, 128), BF),
            pltpu.VMEM((DEVICES, QR, 128), BF),
            pltpu.VMEM((6, WIN, 128), BF),
            pltpu.VMEM((2, WIN, 128), BF),
            pltpu.VMEM((HEADS, TOKENS, 256), BF),
            pltpu.VMEM((3 * HEADS, TOKENS, DV), F32),
            pltpu.VMEM((HEADS, TOKENS, DV), F32),
            pltpu.VMEM((2, 1024, 256), BF),
            pltpu.VMEM((2, 1024, 256), BF),
            pltpu.VMEM((TOKENS, 1024), F32),
            dma((2, 9, 4)),
            dma((2, 9)),
            dma((4,)),
            dma((NZ, 4)),
            dma((2,)),
            dma((4,)),
            dma((8,)),
            dma((5,)),
            dma((5,)),
        ],
        compiler_params=pltpu.CompilerParams(
            collective_id=0, has_side_effects=True, vmem_limit_bytes=VMEM_LIMIT
        ),
    )(sel_ids, *turned)


def solution(mesh):
    in_specs = (
        P("ctx", "grp"),
        P(None, "ctx", "grp"),
        P(None, "ctx", "grp"),
        P("ctx", "grp"),
        P("ctx", "grp"),
        P(None, "grp"),
        P(None, "grp"),
        P(None, "grp"),
        P(None, "grp"),
    )
    return jax.shard_map(body, mesh=mesh, in_specs=in_specs, out_specs=P("ctx", "grp"), check_vma=False)
```
